128 devices in a mesh: grid: 16 (over y, x_hi, core), head: 8 (over x_lo, z).
Axes of the slice: x: 4 (x_hi: 2, x_lo: 2; x = x_hi * 2 + x_lo), y: 4, z: 4, core: 2. Of those that a mesh axis runs over, the one named last changes fastest.
Arguments:
- queries: bfloat16 [65536, 1024], P('grid', 'head'), may hold values from -12 to 12
- resid: bfloat16 [65536, 1024], P('grid', 'head'), may hold values from -6 to 6
- keys: bfloat16 [98304, 1024], P('grid', 'head'), may hold values from -6 to 6
- values: bfloat16 [98304, 1024], P('grid', 'head'), may hold values from -6 to 6
- w_out: bfloat16 [1024, 1024], replicated, may hold values from -0.75 to 0.75
- block_lists: int32 [512, 12], P('grid'), may hold values from 0 to 767, as said below
- block_counts: int32 [512], P('grid'), may hold values from 1 to 12, as said below
Outputs:
- mixed: bfloat16 [65536, 1024], P('grid', 'head')
The draws below stay inside these ranges and needn't reach their ends.
Inputs may be any that keep to these rules, and one draw needn't show every extreme that they name: `block_lists`: each row lists 12 different latent blocks. The blocks listed for grid blocks of the g-th 4096 grid points lie in latent blocks (g - 1) * 48 to (g + 2) * 48 - 1. `block_counts`: entries of a list at positions not below the count are not used.
All inputs are finite; a program needn't handle non-finite values.
Results may differ from the reference program's by a relative error of at most 0.005.
Values may be sent and summed in bfloat16 or wider, within the bound.
A program may use at most 128 MiB of HBM per device.

```python
import math
import jax
import jax.numpy as jnp
from jax import lax

D = 1024
HEADS = 16
BLK = 128
SLOTS = 12
ROWS_DEV = 4096
LB_DEV = 48
GRID = 65536
GBLOCKS = 512
LBLOCKS = 768
LATENT = 98304
N_GRID = 16


def pattern_lists(key):
    base = jax.random.fold_in(key, 11)
    rows = jnp.arange(GBLOCKS, dtype=jnp.int32)
    per_dev = ROWS_DEV // BLK
    owner = rows // per_dev
    center = owner * LB_DEV + rows % per_dev * LB_DEV // per_dev
    low = jnp.clip(center - LB_DEV, 0, LB_DEV * N_GRID - 2 * LB_DEV)
    width = 2 * LB_DEV
    perms = jax.vmap(lambda k: jax.random.permutation(k, width))(jax.random.split(base, GBLOCKS))
    target = jnp.where(rows % 2 == 0, 0, width - 1)
    place = jnp.argmax(perms == target[:, None], axis=1)
    turned = jax.vmap(lambda p, s: jnp.roll(p, -s))(perms, place)
    return (low[:, None] + turned[:, :SLOTS]).astype(jnp.int32)


def latent_keys(key):
    base = jax.random.fold_in(key, 23)
    return jnp.clip(jax.random.normal(base, (LATENT, D), jnp.float32), -6.0, 6.0)


def draw_keys(key, part):
    return latent_keys(key).astype(jnp.bfloat16)


def draw_queries(key, part):
    base = jax.random.fold_in(key, 31)
    return jnp.clip(2.0 * jax.random.normal(base, (GRID, D), jnp.float32), -12.0, 12.0).astype(jnp.bfloat16)


def draw_block_lists(key, part):
    return pattern_lists(key)


def draw_block_counts(key, part):
    base = jax.random.fold_in(key, 47)
    rows = jnp.arange(GBLOCKS, dtype=jnp.int32)
    owner = rows // (ROWS_DEV // BLK)
    polar = (owner < N_GRID // 4) | (owner >= N_GRID - N_GRID // 4)
    lowest = jnp.where(polar, SLOTS // 2, 1)
    drawn = jax.random.randint(base, (GBLOCKS,), lowest, SLOTS + 1)
    drawn = jnp.where(rows % 8 == 0, SLOTS, drawn)
    drawn = jnp.where((rows % 8 == 4) & jnp.logical_not(polar), 1, drawn)
    return drawn.astype(jnp.int32)


def block_levels(key, dims, shards, least, top_value):
    gain, own = 1.0, jax.random.fold_in(key, 6)
    for dim, shards_of in shards:
        steps = jnp.exp(jax.random.uniform(jax.random.fold_in(own, dim), (shards_of,), jnp.float32, least / len(shards), top_value / len(shards)))
        gain = gain * jnp.repeat(steps, dims[dim] // shards_of).reshape([-1 if axis == dim else 1 for axis in range(len(dims))])
    return gain


def scatter_about(rng, shape, spread, bound, cuts=(), kind=jnp.bfloat16):
    entries = jax.random.normal(rng, shape, jnp.float32) * spread
    if len(cuts) > 0:
        entries = block_levels(rng, shape, cuts, -0.22, 0.18) * entries
    return jnp.clip(entries, min=-bound, max=bound).astype(kind)


def setup_inputs(seed: int = 0) -> dict:
    seeds = jax.random.split(jax.random.key(seed), 8)
    queries = draw_queries(jax.random.fold_in(seeds[7], 71), 0)
    resid = scatter_about(seeds[1], (GRID, D), 1.0, 6.0, ((0, 16), (1, 8)))
    keys = draw_keys(jax.random.fold_in(seeds[7], 71), 0)
    values = scatter_about(seeds[3], (LATENT, D), 1.0, 6.0, ((0, 16), (1, 8)))
    w_out = scatter_about(seeds[4], (D, D), (D // 16) ** -0.5, 0.75)
    block_lists = draw_block_lists(jax.random.fold_in(seeds[7], 71), 0)
    block_counts = draw_block_counts(jax.random.fold_in(seeds[7], 71), 0)
    return {"queries": queries, "resid": resid, "keys": keys, "values": values, "w_out": w_out, "block_lists": block_lists, "block_counts": block_counts}


def reference(queries, resid, keys, values, w_out, block_lists, block_counts):
    head_dim = D // HEADS
    scale = 1.0 / math.sqrt(head_dim)
    key_tiles = keys.reshape(LBLOCKS, BLK, D)
    value_tiles = values.reshape(LBLOCKS, BLK, D)

    def one_block(index):
        start = (index * BLK).astype(jnp.int32)
        block_q = lax.dynamic_slice_in_dim(queries, start, BLK, 0).astype(jnp.float32).reshape(BLK, HEADS, head_dim)
        listed = block_lists[index]
        block_k = key_tiles[listed].reshape(SLOTS * BLK, HEADS, head_dim).astype(jnp.float32)
        block_v = value_tiles[listed].reshape(SLOTS * BLK, HEADS, head_dim).astype(jnp.float32)
        live = jnp.arange(SLOTS, dtype=jnp.int32) < block_counts[index]
        usable = jnp.broadcast_to(live[:, None], (SLOTS, BLK)).reshape(SLOTS * BLK)
        score = jnp.einsum('qhd,khd->hqk', block_q, block_k) * scale
        score = jnp.where(usable[None, None, :], score, -1e+30)
        top = lax.optimization_barrier(jnp.max(score, axis=-1, keepdims=True))
        weight = jnp.exp(score - top)
        total = lax.optimization_barrier(jnp.sum(weight, axis=-1, keepdims=True))
        weight_low = weight.astype(jnp.bfloat16).astype(jnp.float32)
        summed = jnp.einsum('hqk,khd->hqd', weight_low, block_v) / total
        return jnp.transpose(summed, (1, 0, 2)).reshape(BLK, D).astype(jnp.bfloat16)
    attended = lax.map(one_block, jnp.arange(GBLOCKS, dtype=jnp.int32)).reshape(GRID, D)
    projected = jnp.dot(attended, w_out, preferred_element_type=jnp.float32)
    return (resid.astype(jnp.float32) + projected).astype(jnp.bfloat16)
```

```python
import functools
import math

import jax
import jax.numpy as jnp
from jax import lax
from jax.experimental import pallas as pl
from jax.experimental.pallas import tpu as pltpu
from jax.sharding import PartitionSpec as P

D = 1024
HEADS = 16
HEAD_DIM = D // HEADS
BLK = 128
SLOTS = 12
ROW = 16
QUAD = 4
OUT = BLK + 16
LOG2 = math.log2(math.e) / math.sqrt(HEAD_DIM)
LOW = -1e30


def owner_lists(block_lists, block_counts, per_device):
    first = (lax.axis_index("grid") - 1) * per_device
    ids = block_lists - first
    slot = jnp.arange(SLOTS, dtype=jnp.int32)
    live = slot[None, :] < block_counts[:, None]
    out = []
    for owner in range(3):
        here = ids - owner * per_device
        mine = live & (here >= 0) & (here < per_device)
        before = slot[:, None] < slot[None, :]
        place = jnp.sum(mine[:, :, None] & before[None], axis=1, dtype=jnp.int32)
        hit = mine[:, :, None] & (place[:, :, None] == jnp.arange(ROW)[None, None, :])
        packed = jnp.sum(jnp.where(hit, here[:, :, None], 0), axis=1)
        count = jnp.sum(mine, axis=1, dtype=jnp.int32)
        out.append(jnp.where(jnp.arange(ROW)[None, :] == SLOTS, count[:, None], packed))
    return jnp.stack(out)


def partial_kernel(make_vt, lists, q_ref, k_ref, v_ref, o_ref, *rest):
    if make_vt:
        vt, steps, s_ref, acc_ref = rest
    else:
        vt = v_ref
        steps, s_ref, acc_ref = rest
    blocks = o_ref.shape[0]
    if make_vt:

        def turn(c, carry):
            vt[c, 0:BLK, :] = v_ref[pl.ds(pl.multiple_of(c * BLK, BLK), BLK), :].T
            vt[c, BLK:OUT, :] = jnp.ones((OUT - BLK, BLK), jnp.bfloat16)
            return carry

        lax.fori_loop(0, vt.shape[0], turn, 0, unroll=4)

    def clear(b, at):
        o_ref[b] = jnp.zeros((OUT, BLK), jnp.bfloat16)
        for t in range(SLOTS // QUAD):
            steps[at + t] = b * 4 + t
        return at + (lists[b * ROW + SLOTS] + QUAD - 1) // QUAD

    steps[0] = 0
    total = lax.fori_loop(0, blocks, clear, jnp.int32(0))
    last = steps[jnp.maximum(total - 1, 0)]
    for t in range(3):
        steps[total + t] = last // 4 * 4 + 3
    acc_ref[...] = jnp.zeros_like(acc_ref)
    row128 = lax.broadcasted_iota(jnp.int32, (BLK, BLK), 0)
    row16 = lax.broadcasted_iota(jnp.int32, (OUT - BLK, BLK), 0)

    def ids_of(t):
        step = steps[t]
        b, part = step // 4, step % 4
        base = b * ROW
        count = lists[base + SLOTS]
        ids = [lists[base + jnp.minimum(part * QUAD + j, SLOTS - 1)] for j in range(QUAD)]
        dead = [part * QUAD + j >= count for j in range(QUAD)]
        return b, part, ids, dead

    def score(t, par, m_before):
        b, part, ids, dead = ids_of(t)
        qt = q_ref[pl.ds(pl.multiple_of(b * BLK, BLK), BLK), :].T
        zero = jnp.zeros_like(qt)
        q_both = jnp.concatenate(
            [jnp.where(row128 < HEAD_DIM, qt, zero), jnp.where(row128 >= HEAD_DIM, qt, zero)], axis=1
        )
        top = None
        for j in range(QUAD):
            keys = k_ref[pl.ds(pl.multiple_of(ids[j] * BLK, BLK), BLK), :]
            s = jnp.dot(keys, q_both, preferred_element_type=jnp.float32)
            s_ref[par, pl.ds(j * BLK, BLK), :] = s
            m = jnp.max(s.reshape(BLK // 8, 8, 2 * BLK), axis=0)
            m = jnp.where(dead[j], LOW, m)
            top = m if top is None else jnp.maximum(top, m)
        top = jnp.max(top, axis=0, keepdims=True) * LOG2
        top = top.astype(jnp.bfloat16).astype(jnp.float32)
        m_before = jnp.where(part == 0, LOW, m_before)
        m_now = jnp.maximum(m_before, top)
        return m_now, jnp.exp2(m_before - m_now)

    def weigh(t, par, m_now, fade):
        b, part, ids, dead = ids_of(t)
        both = None
        for j in range(0, QUAD, 2):
            w = []
            for i in (j, j + 1):
                shift = m_now + jnp.where(dead[i], -LOW, 0.0)
                w.append(
                    jnp.exp2(s_ref[par, pl.ds(i * BLK, BLK), :] * LOG2 - shift).astype(jnp.bfloat16)
                )
            vals = jnp.concatenate([vt[ids[j]], vt[ids[j + 1]]], axis=1)
            d = jnp.dot(vals, jnp.concatenate(w, axis=0), preferred_element_type=jnp.float32)
            both = d if both is None else both + d
        acc0 = acc_ref[0:HEAD_DIM] * fade[:, :BLK] + both[0:HEAD_DIM, :BLK]
        acc1 = acc_ref[HEAD_DIM:BLK] * fade[:, BLK:] + both[HEAD_DIM:BLK, BLK:]
        sum0 = acc_ref[BLK : BLK + 8] * fade[:, :BLK] + both[BLK : BLK + 8, :BLK]
        sum1 = acc_ref[BLK + 8 : OUT] * fade[:, BLK:] + both[BLK : BLK + 8, BLK:]
        acc_ref[0:HEAD_DIM] = acc0
        acc_ref[HEAD_DIM:BLK] = acc1
        acc_ref[BLK : BLK + 8] = sum0
        acc_ref[BLK + 8 : OUT] = sum1
        o_ref[b, 0:HEAD_DIM] = acc0.astype(jnp.bfloat16)
        o_ref[b, HEAD_DIM:BLK] = acc1.astype(jnp.bfloat16)
        high0 = sum0.astype(jnp.bfloat16).astype(jnp.float32)
        high1 = sum1.astype(jnp.bfloat16).astype(jnp.float32)
        stats = jnp.zeros((OUT - BLK, BLK), jnp.float32)
        for i, line in enumerate(
            (m_now[:, :BLK], high0[0:1], (sum0 - high0)[0:1], m_now[:, BLK:], high1[0:1], (sum1 - high1)[0:1])
        ):
            stats = jnp.where(row16 == i, line, stats)
        o_ref[b, BLK:OUT] = stats.astype(jnp.bfloat16)

    start = jnp.full((1, 2 * BLK), LOW, jnp.float32)
    m0, f0 = score(0, 0, start)

    def pair(i, carry):
        m0, f0 = carry
        t = 2 * i
        m1, f1 = score(t + 1, 1, m0)
        weigh(t, 0, m0, f0)
        m2, f2 = score(t + 2, 0, m1)
        weigh(t + 1, 1, m1, f1)
        return m2, f2

    lax.fori_loop(0, (total + 1) // 2, pair, (m0, f0))


def partial(lists, q, k, v, make_vt, name, blocks):
    per_device = k.shape[0] // BLK
    shapes = [jax.ShapeDtypeStruct((blocks, OUT, BLK), jnp.bfloat16)]
    if make_vt:
        shapes.append(jax.ShapeDtypeStruct((per_device, OUT, BLK), jnp.bfloat16))
    vmem = pl.BlockSpec(memory_space=pltpu.VMEM)
    return pl.pallas_call(
        functools.partial(partial_kernel, make_vt),
        out_shape=shapes,
        in_specs=[pl.BlockSpec(memory_space=pltpu.SMEM), vmem, vmem, vmem],
        out_specs=[vmem] * len(shapes),
        scratch_shapes=[
            pltpu.SMEM((blocks * 3 + 8,), jnp.int32),
            pltpu.VMEM((2, QUAD * BLK, 2 * BLK), jnp.float32),
            pltpu.VMEM((OUT, BLK), jnp.float32),
        ],
        compiler_params=pltpu.CompilerParams(vmem_limit_bytes=32 << 20),
        cost_estimate=pl.CostEstimate(flops=8_000_000_000, bytes_accessed=6 << 20, transcendentals=5_000_000),
        name=name,
    )(lists, q, k, v)


def combine_kernel(own, left, right, o_ref):
    def one(b, carry):
        parts = (own[b], left[b], right[b])
        stats = [p[BLK:OUT].astype(jnp.float32) for p in parts]
        heads = []
        for h in range(2):
            sums = [s[3 * h + 1 : 3 * h + 2] + s[3 * h + 2 : 3 * h + 3] for s in stats]
            tops = [jnp.where(l > 0, s[3 * h : 3 * h + 1], LOW) for s, l in zip(stats, sums)]
            top = jnp.maximum(jnp.maximum(tops[0], tops[1]), tops[2])
            scale = [jnp.exp2(t - top) for t in tops]
            total = sum(l * c for l, c in zip(sums, scale))
            rows = slice(h * HEAD_DIM, (h + 1) * HEAD_DIM)
            heads.append(sum(p[rows].astype(jnp.float32) * (c / total) for p, c in zip(parts, scale)))
        both = jnp.concatenate(heads, axis=0).T
        o_ref[pl.ds(pl.multiple_of(b * BLK, BLK), BLK), :] = both.astype(jnp.bfloat16)
        return carry

    lax.fori_loop(0, own.shape[0], one, 0, unroll=4)


def combine(own, left, right):
    vmem = pl.BlockSpec(memory_space=pltpu.VMEM)
    return pl.pallas_call(
        combine_kernel,
        out_shape=jax.ShapeDtypeStruct((own.shape[0] * BLK, BLK), jnp.bfloat16),
        in_specs=[vmem] * 3,
        out_specs=vmem,
        compiler_params=pltpu.CompilerParams(vmem_limit_bytes=32 << 20),
        name="combine",
    )(own, left, right)


def local(queries, resid, keys, values, w_out, block_lists, block_counts):
    blocks = queries.shape[0] // BLK
    per_device = keys.shape[0] // BLK
    lists = owner_lists(block_lists, block_counts, per_device)
    coded = lists.astype(jnp.bfloat16).reshape(-1, BLK)
    coded = jnp.pad(coded, ((0, 16 - coded.shape[0]), (0, 0)))
    packed = jnp.concatenate([queries, coded], axis=0)
    count = lax.axis_size("grid")
    up = [(i, i + 1) for i in range(count - 1)]
    down = [(i + 1, i) for i in range(count - 1)]
    from_left = lax.ppermute(packed, "grid", up)
    from_right = lax.ppermute(packed, "grid", down)
    own, vt = partial(lists[1].reshape(-1), queries, keys, values, True, "own_part", blocks)

    def lists_in(got, owner):
        rows = 3 * blocks * ROW // BLK
        got = lax.slice_in_dim(got, blocks * BLK, blocks * BLK + rows, axis=0)
        return got.astype(jnp.int32).reshape(3, -1)[owner]

    [for_left] = partial(lists_in(from_left, 2), from_left, keys, vt, False, "left_part", blocks)
    left_back = lax.ppermute(for_left, "grid", down)
    [for_right] = partial(lists_in(from_right, 0), from_right, keys, vt, False, "right_part", blocks)
    right_back = lax.ppermute(for_right, "grid", up)
    attended = combine(own, left_back, right_back)
    arrived = lax.all_to_all(attended, "head", split_axis=0, concat_axis=1, tiled=True)
    projected = jnp.dot(arrived, w_out, preferred_element_type=jnp.float32).astype(jnp.bfloat16)
    home = lax.all_to_all(projected, "head", split_axis=1, concat_axis=0, tiled=True)
    return (resid.astype(jnp.float32) + home.astype(jnp.float32)).astype(jnp.bfloat16)


def solution(mesh):
    placed = (
        P("grid", "head"),
        P("grid", "head"),
        P("grid", "head"),
        P("grid", "head"),
        P(),
        P("grid", None),
        P("grid"),
    )
    return jax.shard_map(
        local, mesh=mesh, in_specs=placed, out_specs=P("grid", "head"), check_vma=False
    )
```

```python
import functools
import math

import jax
import jax.numpy as jnp
from jax import lax
from jax.experimental import pallas as pl
from jax.experimental.pallas import tpu as pltpu
from jax.sharding import PartitionSpec as P

D = 1024
HEADS = 16
HEAD_DIM = D // HEADS
BLK = 128
SLOTS = 12
ROW = 16
QUAD = 4
OUT = BLK + 16
LOG2 = math.log2(math.e) / math.sqrt(HEAD_DIM)
LOW = -1e30
SUBS = 2
BF16, F32, I32 = jnp.bfloat16, jnp.float32, jnp.int32
MESH = pl.DeviceIdType.MESH


def rows(b, size=BLK):
    return pl.ds(pl.multiple_of(b * size, size), size)


def entry(lists, b, j):
    return lists[b // (BLK // ROW), b % (BLK // ROW) * ROW + j]


def place():
    count = lax.axis_size("grid")
    g = lax.axis_index("grid")
    core = lax.rem(g, 2)
    return g, core, g + 1 - 2 * core, lax.rem(g - 1 + 2 * core + count, count)


def both_heads(q):
    qt = q.T
    row = lax.broadcasted_iota(I32, (BLK, BLK), 0)
    zero = jnp.zeros_like(qt)
    return jnp.concatenate([jnp.where(row < HEAD_DIM, qt, zero), jnp.where(row >= HEAD_DIM, qt, zero)], axis=1)


def score_slots(q, k_ref, s_ref, par, ids, bias):
    q_both = both_heads(q)
    top = None
    for j, (c, less) in enumerate(zip(ids, bias)):
        s = jnp.dot(k_ref[c], q_both, preferred_element_type=F32)
        s_ref[par, pl.ds(j * BLK, BLK), :] = s
        m = jnp.max(s.reshape(BLK // 8, 8, 2 * BLK), axis=0)
        m = m - less
        top = m if top is None else jnp.maximum(top, m)
    top = jnp.max(top, axis=0, keepdims=True) * LOG2
    return top.astype(BF16).astype(F32)


def weigh_slots(s_ref, par, vt, ids, bias, top):
    both = None
    for j in range(0, len(ids), 2):
        w = []
        for i in (j, j + 1):
            shift = top + bias[i]
            w.append(jnp.exp2(s_ref[par, pl.ds(i * BLK, BLK), :] * LOG2 - shift).astype(BF16))
        vals = jnp.concatenate([vt[ids[j]], vt[ids[j + 1]]], axis=1)
        d = jnp.dot(vals, jnp.concatenate(w, axis=0), preferred_element_type=F32)
        both = d if both is None else both + d
    return both


def put_result(o_ref, b, acc0, acc1, top, sum0, sum1):
    o_ref[b, 0:HEAD_DIM] = acc0.astype(BF16)
    o_ref[b, HEAD_DIM:BLK] = acc1.astype(BF16)
    row = lax.broadcasted_iota(I32, (OUT - BLK, BLK), 0)
    high0 = sum0.astype(BF16).astype(F32)
    high1 = sum1.astype(BF16).astype(F32)
    stats = jnp.zeros((OUT - BLK, BLK), F32)
    lines = (top[:, :BLK], high0[0:1], (sum0 - high0)[0:1], top[:, BLK:], high1[0:1], (sum1 - high1)[0:1])
    for i, line in enumerate(lines):
        stats = jnp.where(row == i, line, stats)
    o_ref[b, BLK:OUT] = stats.astype(BF16)


def turn_values(v_ref, vt, first, count):
    def turn(i, carry):
        c = first + i
        vt[c, 0:BLK, :] = v_ref[c].T
        vt[c, BLK:OUT, :] = jnp.ones((OUT - BLK, BLK), BF16)
        return carry

    lax.fori_loop(0, count, turn, 0, unroll=4)


def chip_kernel(
    ids_s, bias_s, lists_h, q_h, k_h, v_h, o_ref, vt_o, qx_o, lx_o, q_ref, k_all, v_all, vt, s_ref, local_sem, send_sem, recv_sem
):
    blocks = o_ref.shape[0]
    per_device = vt_o.shape[0]
    head = lax.axis_index("head")
    g, core, mate, cross = place()
    barrier = pltpu.get_barrier_semaphore()
    for other in (mate, cross):
        pl.semaphore_signal(barrier, inc=1, device_id=(other, head), device_id_type=MESH)
    pl.semaphore_wait(barrier, 2)

    mine = pl.ds(core * per_device, per_device)

    def remote(i, src, dst, other):
        return pltpu.make_async_remote_copy(
            src_ref=src, dst_ref=dst, send_sem=send_sem.at[i], recv_sem=recv_sem.at[i],
            device_id=(other, head), device_id_type=MESH,
        )

    out_v = remote(0, v_h, v_all.at[mine], mate)
    out_k = remote(1, k_h, k_all.at[mine], mate)
    out_q = remote(2, q_h, qx_o, cross)
    out_l = remote(3, lists_h, lx_o, cross)
    in_v = pltpu.make_async_copy(v_h, v_all.at[mine], local_sem.at[0])
    in_k = pltpu.make_async_copy(k_h, k_all.at[mine], local_sem.at[1])
    in_q = pltpu.make_async_copy(q_h, q_ref, local_sem.at[2])
    for copy in (out_v, in_v, out_q, out_k, in_k, in_q, out_l):
        copy.start()
    in_v.wait()
    turn_values(v_all, vt, core * per_device, per_device)
    keep_vt = pltpu.make_async_copy(vt.at[pl.ds(core * per_device, per_device)], vt_o, local_sem.at[3])
    keep_vt.start()
    out_v.wait_recv()
    turn_values(v_all, vt, (1 - core) * per_device, per_device)
    in_k.wait()
    in_q.wait()
    out_k.wait_recv()

    def ids_of(b):
        return [entry(ids_s, b, j) for j in range(SLOTS)], [entry(bias_s, b, j) for j in range(SLOTS)]

    def score(b, par):
        ids, bias = ids_of(b)
        return score_slots(q_ref[rows(b), :], k_all, s_ref, par, ids, bias)

    def weigh(b, par, top):
        ids, bias = ids_of(b)
        both = weigh_slots(s_ref, par, vt, ids, bias, top)
        sums = both[BLK : BLK + 8]
        put_result(o_ref, b, both[0:HEAD_DIM, :BLK], both[HEAD_DIM:BLK, BLK:], top, sums[:, :BLK], sums[:, BLK:])

    def pair(i, m0):
        b = 2 * i
        m1 = score(b + 1, 1)
        weigh(b, 0, m0)
        m2 = score(jnp.minimum(b + 2, blocks - 1), 0)
        weigh(b + 1, 1, m1)
        return m2

    lax.fori_loop(0, blocks // 2, pair, score(0, 0))
    keep_vt.wait()
    out_v.wait_send()
    out_k.wait_send()
    out_q.wait()
    out_l.wait()


def chip_part(ids, bias, lists, q, k, v):
    blocks, per_device = q.shape[0] // BLK, k.shape[0]
    vmem = pl.BlockSpec(memory_space=pltpu.VMEM)
    any_ = pl.BlockSpec(memory_space=pl.ANY)
    return pl.pallas_call(
        chip_kernel,
        out_shape=[
            jax.ShapeDtypeStruct((blocks, OUT, BLK), BF16),
            jax.ShapeDtypeStruct((per_device, OUT, BLK), BF16),
            jax.ShapeDtypeStruct(q.shape, BF16),
            jax.ShapeDtypeStruct(lists.shape, I32),
        ],
        in_specs=[pl.BlockSpec(memory_space=pltpu.SMEM)] * 2 + [any_] * 4,
        out_specs=[vmem, any_, any_, any_],
        scratch_shapes=[
            pltpu.VMEM(q.shape, BF16),
            pltpu.VMEM((2 * per_device, BLK, BLK), BF16),
            pltpu.VMEM((2 * per_device, BLK, BLK), BF16),
            pltpu.VMEM((2 * per_device, OUT, BLK), BF16),
            pltpu.VMEM((2, SLOTS * BLK, 2 * BLK), F32),
            pltpu.SemaphoreType.DMA((4,)),
            pltpu.SemaphoreType.DMA((4,)),
            pltpu.SemaphoreType.DMA((4,)),
        ],
        compiler_params=pltpu.CompilerParams(vmem_limit_bytes=40 << 20, collective_id=0, has_side_effects=True),
        cost_estimate=pl.CostEstimate(flops=8_000_000_000, bytes_accessed=12 << 20, transcendentals=12_000_000),
        name="chip_part",
    )(ids, bias, lists, q, k, v)


def cross_kernel(lists, q_h, k_h, vt_h, o_ref, q_ref, k_ref, vt, found, steps, s_ref, acc_ref, sem):
    loads = [
        pltpu.make_async_copy(src, dst, sem.at[i])
        for i, (src, dst) in enumerate(((q_h, q_ref), (k_h, k_ref), (vt_h, vt)))
    ]
    for load in loads:
        load.start()
    blocks = o_ref.shape[0]
    per_device = vt.shape[0]
    low = lax.axis_index("grid") * per_device

    def search(b, at):
        count = entry(lists, b, SLOTS)
        n = jnp.int32(0)
        for j in range(SLOTS):
            c = entry(lists, b, j) - low
            found[b * ROW + n] = c
            hit = (c >= 0) & (c < per_device) & (j < count)
            n = n + hit.astype(I32)
        for j in range(QUAD - 1):
            found[b * ROW + n + j] = 0
        found[b * ROW + ROW - 1] = n
        for t in range(SLOTS // QUAD):
            steps[at + t] = b * 4 + t
        o_ref[b] = jnp.zeros((OUT, BLK), BF16)
        return at + (n + QUAD - 1) // QUAD

    steps[0] = 0
    total = lax.fori_loop(0, blocks, search, jnp.int32(0))
    last = steps[jnp.maximum(total - 1, 0)]
    for t in range(5):
        steps[total + t] = last // 4 * 4 + 3
    acc_ref[...] = jnp.zeros_like(acc_ref)
    for load in loads:
        load.wait()

    def ids_of(t):
        b, part = steps[t] // 4, steps[t] % 4
        count = found[b * ROW + ROW - 1]
        dead = [part * QUAD + j >= count for j in range(QUAD)]
        ids = [jnp.where(gone, 0, found[b * ROW + part * QUAD + j]) for j, gone in enumerate(dead)]
        return b, part, ids, [jnp.where(gone, -LOW, 0.0) for gone in dead]

    def score(t, par, before):
        b, part, ids, bias = ids_of(t)
        top = score_slots(q_ref[rows(b), :], k_ref, s_ref, par, ids, bias)
        before = jnp.where(part == 0, LOW, before)
        top = jnp.maximum(before, top)
        return top, jnp.exp2(before - top)

    def weigh(t, par, top, fade):
        b, part, ids, bias = ids_of(t)
        both = weigh_slots(s_ref, par, vt, ids, bias, top)
        acc0 = acc_ref[0:HEAD_DIM] * fade[:, :BLK] + both[0:HEAD_DIM, :BLK]
        acc1 = acc_ref[HEAD_DIM:BLK] * fade[:, BLK:] + both[HEAD_DIM:BLK, BLK:]
        sum0 = acc_ref[BLK : BLK + 8] * fade[:, :BLK] + both[BLK : BLK + 8, :BLK]
        sum1 = acc_ref[BLK + 8 : OUT] * fade[:, BLK:] + both[BLK : BLK + 8, BLK:]
        acc_ref[0:HEAD_DIM] = acc0
        acc_ref[HEAD_DIM:BLK] = acc1
        acc_ref[BLK : BLK + 8] = sum0
        acc_ref[BLK + 8 : OUT] = sum1
        put_result(o_ref, b, acc0, acc1, top, sum0, sum1)

    def four(i, carry):
        now = carry
        for j in range(4):
            t = 4 * i + j
            then = score(t + 1, (j + 1) % 4, now[0])
            weigh(t, j, *now)
            now = then
        return now

    start = jnp.full((1, 2 * BLK), LOW, F32)
    lax.fori_loop(0, (total + 3) // 4, four, score(0, 0, start))


def cross_part(lists, q, k, vt):
    blocks = q.shape[0] // BLK
    any_ = pl.BlockSpec(memory_space=pl.ANY)
    return pl.pallas_call(
        cross_kernel,
        out_shape=jax.ShapeDtypeStruct((blocks, OUT, BLK), BF16),
        in_specs=[pl.BlockSpec(memory_space=pltpu.SMEM), any_, any_, any_],
        out_specs=pl.BlockSpec(memory_space=pltpu.VMEM),
        scratch_shapes=[
            pltpu.VMEM(q.shape, BF16),
            pltpu.VMEM(k.shape, BF16),
            pltpu.VMEM(vt.shape, BF16),
            pltpu.SMEM((blocks * ROW,), I32),
            pltpu.SMEM((blocks * 3 + 8,), I32),
            pltpu.VMEM((4, QUAD * BLK, 2 * BLK), F32),
            pltpu.VMEM((OUT, BLK), F32),
            pltpu.SemaphoreType.DMA((3,)),
        ],
        compiler_params=pltpu.CompilerParams(vmem_limit_bytes=32 << 20),
        name="cross_part",
    )(lists, q, k, vt)


def combine(parts):
    stats = [p[BLK:OUT].astype(F32) for p in parts]
    heads = []
    for h in range(2):
        sums = [s[3 * h + 1 : 3 * h + 2] + s[3 * h + 2 : 3 * h + 3] for s in stats]
        tops = [jnp.where(l > 0, s[3 * h : 3 * h + 1], LOW) for s, l in zip(stats, sums)]
        top = functools.reduce(jnp.maximum, tops)
        scale = [jnp.exp2(t - top) for t in tops]
        total = sum(l * c for l, c in zip(sums, scale))
        part = slice(h * HEAD_DIM, (h + 1) * HEAD_DIM)
        heads.append(sum(p[part].astype(F32) * (c / total) for p, c in zip(parts, scale)))
    return jnp.concatenate(heads, axis=0).T.astype(BF16)


def project_kernel(own, other, w_h, home, got, att, w_ref, stage, w_sem, own_sem, send_sem, recv_sem, back_sem, home_sem):
    heads = lax.axis_size("head")
    head = lax.axis_index("head")
    g, core, mate, cross = place()
    blocks = own.shape[0] // heads
    per_sub = blocks // SUBS
    load_w = pltpu.make_async_copy(w_h, w_ref, w_sem)
    load_w.start()
    barrier = pltpu.get_barrier_semaphore()
    for i in range(1, heads):
        pl.semaphore_signal(barrier, inc=1, device_id=(g, lax.rem(head + i, heads)), device_id_type=MESH)
    for i in range(heads):
        pl.semaphore_signal(barrier, inc=1, device_id=(cross, lax.rem(head + i, heads)), device_id_type=MESH)
    pl.semaphore_wait(barrier, 2 * heads - 1)

    def to_own(s, i):
        to = lax.rem(head + i, heads)
        return pltpu.make_async_remote_copy(
            src_ref=own.at[pl.ds(to * blocks + s * per_sub, per_sub)],
            dst_ref=got.at[0, i, pl.ds(s * per_sub, per_sub)],
            send_sem=send_sem.at[0, s, i], recv_sem=recv_sem.at[0, s, i],
            device_id=(g, to), device_id_type=MESH,
        )

    def to_cross(s, i):
        to = lax.rem(head + i, heads)
        return pltpu.make_async_remote_copy(
            src_ref=other.at[pl.ds(to * blocks + s * per_sub, per_sub)],
            dst_ref=got.at[1, i, pl.ds(s * per_sub, per_sub)],
            send_sem=send_sem.at[1, s, i], recv_sem=recv_sem.at[1, s, i],
            device_id=(cross, to), device_id_type=MESH,
        )

    keep = pltpu.make_async_copy(own.at[pl.ds(head * blocks, blocks)], got.at[0, 0], own_sem)
    keep.start()
    for s in range(SUBS):
        for i in range(heads):
            to_cross(s, i).start()
            if i:
                to_own(s, i).start()
    keep.wait()
    load_w.wait()

    def back(s, i):
        to = lax.rem(head + i, heads)
        return pltpu.make_async_remote_copy(
            src_ref=stage.at[to, pl.ds(s * per_sub * BLK, per_sub * BLK)],
            dst_ref=home.at[pl.ds(pl.multiple_of(head * blocks * BLK, BLK) + s * per_sub * BLK, per_sub * BLK)],
            send_sem=back_sem.at[s, i], recv_sem=home_sem.at[s, i],
            device_id=(g, to), device_id_type=MESH,
        )

    for s in range(SUBS):
        for i in range(heads):
            to_cross(s, i).wait_recv()
            if i:
                to_own(s, i).wait_recv()
            source = lax.rem(head - i + heads, heads)
            for n in range(per_sub):
                b = s * per_sub + n
                att[pl.ds(b * BLK, BLK), rows(source)] = combine((got[0, i, b], got[1, i, b]))
        size = per_sub * BLK
        for n in range(0, D, 256):
            out = jnp.dot(att[pl.ds(s * size, size), :], w_ref[:, n : n + 256], preferred_element_type=F32).astype(BF16)
            for c in range(2):
                stage[n // BLK + c, pl.ds(s * size, size), :] = out[:, c * BLK : (c + 1) * BLK]
        for i in range(1, heads):
            back(s, i).start()
        home[pl.ds(pl.multiple_of(head * blocks * BLK, BLK) + s * size, size), :] = stage[head, pl.ds(s * size, size), :]
    for s in range(SUBS):
        for i in range(heads):
            to_cross(s, i).wait_send()
            if i:
                to_own(s, i).wait_send()
                back(s, i).wait()


def project(own, other, w_out):
    heads = lax.axis_size("head")
    blocks = own.shape[0] // heads
    vmem = pl.BlockSpec(memory_space=pltpu.VMEM)
    return pl.pallas_call(
        project_kernel,
        out_shape=jax.ShapeDtypeStruct((own.shape[0] * BLK, BLK), BF16),
        in_specs=[vmem, vmem, pl.BlockSpec(memory_space=pl.ANY)],
        out_specs=vmem,
        scratch_shapes=[
            pltpu.VMEM((2, heads, blocks, OUT, BLK), BF16),
            pltpu.VMEM((blocks * BLK, D), BF16),
            pltpu.VMEM((D, D), BF16),
            pltpu.VMEM((heads, blocks * BLK, BLK), BF16),
            pltpu.SemaphoreType.DMA,
            pltpu.SemaphoreType.DMA,
            pltpu.SemaphoreType.DMA((2, SUBS, heads)),
            pltpu.SemaphoreType.DMA((2, SUBS, heads)),
            pltpu.SemaphoreType.DMA((SUBS, heads)),
            pltpu.SemaphoreType.DMA((SUBS, heads)),
        ],
        compiler_params=pltpu.CompilerParams(vmem_limit_bytes=32 << 20, collective_id=1, has_side_effects=True),
        name="project",
    )(own, other, w_out)


def local(queries, resid, keys, values, w_out, block_lists, block_counts):
    per_device = keys.shape[0] // BLK
    keys, values = keys.reshape(-1, BLK, BLK), values.reshape(-1, BLK, BLK)

    def table(a):
        return jnp.pad(a, ((0, 8 * BLK // ROW - a.shape[0]), (0, ROW - a.shape[1]))).reshape(8, BLK)

    g = lax.axis_index("grid")
    near = block_lists - (g - lax.rem(g, 2)) * per_device
    used = jnp.arange(SLOTS, dtype=jnp.int32)[None, :] < block_counts[:, None]
    used &= (near >= 0) & (near < 2 * per_device)
    ids, bias = table(jnp.where(used, near, 0)), table(jnp.where(used, 0.0, -LOW).astype(jnp.float32))
    lists = table(jnp.concatenate([block_lists, block_counts[:, None]], axis=1))
    own, vt, cross_q, cross_lists = chip_part(ids, bias, lists, queries, keys, values)
    other = cross_part(cross_lists, cross_q, keys, vt)
    home = project(own, other, w_out)
    return (resid.astype(jnp.float32) + home.astype(jnp.float32)).astype(jnp.bfloat16)


def solution(mesh):
    placed = (
        P("grid", "head"),
        P("grid", "head"),
        P("grid", "head"),
        P("grid", "head"),
        P(),
        P("grid", None),
        P("grid"),
    )
    return jax.shard_map(
        local, mesh=mesh, in_specs=placed, out_specs=P("grid", "head"), check_vma=False
    )
```

```python
import functools
import math

import jax
import jax.numpy as jnp
from jax import lax
from jax.experimental import pallas as pl
from jax.experimental.pallas import tpu as pltpu
from jax.sharding import PartitionSpec as P

D = 1024
HEADS = 16
HEAD_DIM = D // HEADS
BLK = 128
SLOTS = 12
ROW = 16
OUT = BLK + 16
LOG2 = math.log2(math.e) / math.sqrt(HEAD_DIM)
LOW = -1e30
SUBLINES = 4
SUBS = 2
BF16, F32, I32 = jnp.bfloat16, jnp.float32, jnp.int32
MESH = pl.DeviceIdType.MESH


def rows(b, size=BLK):
    return pl.ds(pl.multiple_of(b * size, size), size)


def place():
    count = lax.axis_size("grid")
    g = lax.axis_index("grid")
    core = lax.rem(g, 2)
    return g, core, g + 1 - 2 * core, lax.rem(g - 1 + 2 * core + count, count)


def both_heads(q):
    qt = q.T
    row = lax.broadcasted_iota(I32, (BLK, BLK), 0)
    zero = jnp.zeros_like(qt)
    return jnp.concatenate([jnp.where(row < HEAD_DIM, qt, zero), jnp.where(row >= HEAD_DIM, qt, zero)], axis=1)


def score_slots(q, k_ref, s_ref, par, ids, bias):
    q_both = both_heads(q)
    top = None
    for j, (c, less) in enumerate(zip(ids, bias)):
        s = jnp.dot(k_ref[c], q_both, preferred_element_type=F32)
        s_ref[par, pl.ds(j * BLK, BLK), :] = s
        m = jnp.max(s.reshape(BLK // 8, 8, 2 * BLK), axis=0)
        m = m - less
        top = m if top is None else jnp.maximum(top, m)
    top = jnp.max(top, axis=0, keepdims=True) * LOG2
    return top.astype(BF16).astype(F32)


def weigh_slots(s_ref, par, vt, ids, bias, top):
    both = None
    for j in range(0, len(ids), 2):
        w = []
        for i in (j, j + 1):
            shift = top + bias[i]
            w.append(jnp.exp2(s_ref[par, pl.ds(i * BLK, BLK), :] * LOG2 - shift).astype(BF16))
        vals = jnp.concatenate([vt[ids[j]], vt[ids[j + 1]]], axis=1)
        d = jnp.dot(vals, jnp.concatenate(w, axis=0), preferred_element_type=F32)
        both = d if both is None else both + d
    return both


def put_result(o_ref, b, acc0, acc1, top, sum0, sum1):
    o_ref[b, 0:HEAD_DIM] = acc0.astype(BF16)
    o_ref[b, HEAD_DIM:BLK] = acc1.astype(BF16)
    row = lax.broadcasted_iota(I32, (OUT - BLK, BLK), 0)
    high0 = sum0.astype(BF16).astype(F32)
    high1 = sum1.astype(BF16).astype(F32)
    stats = jnp.zeros((OUT - BLK, BLK), F32)
    lines = (top[:, :BLK], high0[0:1], (sum0 - high0)[0:1], top[:, BLK:], high1[0:1], (sum1 - high1)[0:1])
    for i, line in enumerate(lines):
        stats = jnp.where(row == i, line, stats)
    o_ref[b, BLK:OUT] = stats.astype(BF16)


def turn_values(v_ref, vt, first, count):
    def turn(i, carry):
        c = first + i
        vt[c, 0:BLK, :] = v_ref[c].T
        vt[c, BLK:OUT, :] = jnp.ones((OUT - BLK, BLK), BF16)
        return carry

    lax.fori_loop(0, count, turn, 0, unroll=4)


def combine(parts):
    stats = [p[BLK:OUT].astype(F32) for p in parts]
    heads = []
    for h in range(2):
        sums = [s[3 * h + 1 : 3 * h + 2] + s[3 * h + 2 : 3 * h + 3] for s in stats]
        tops = [jnp.where(l > 0, s[3 * h : 3 * h + 1], LOW) for s, l in zip(stats, sums)]
        top = functools.reduce(jnp.maximum, tops)
        scale = [jnp.exp2(t - top) for t in tops]
        total = sum(l * c for l, c in zip(sums, scale))
        part = slice(h * HEAD_DIM, (h + 1) * HEAD_DIM)
        heads.append(sum(p[part].astype(F32) * (c / total) for p, c in zip(parts, scale)))
    return jnp.concatenate(heads, axis=0).T.astype(BF16)


def mixed_kernel(
    tables, q_h, k_h, v_h, w_h, home, lists_o,
    tab, q_all, k_all, v_all, vt, s_ref, done, got, att, w_ref, stage,
    tab_sem, load_sem, pair_send, pair_recv, q_send, q_recv, part_send, part_recv, back_send, back_recv,
):
    heads = lax.axis_size("head")
    head = lax.axis_index("head")
    g, core, mate, cross = place()
    per_device = k_h.shape[0]
    blocks = q_h.shape[0] // BLK // heads
    load_w = pltpu.make_async_copy(w_h, w_ref, load_sem.at[0])
    mine = pl.ds(core * per_device, per_device)
    in_v = pltpu.make_async_copy(v_h, v_all.at[mine], load_sem.at[1])
    in_k = pltpu.make_async_copy(k_h, k_all.at[mine], load_sem.at[2])
    in_q = pltpu.make_async_copy(q_h, q_all.at[0], load_sem.at[3])
    in_t = pltpu.make_async_copy(tables.at[0], tab.at[0], tab_sem.at[0])
    for load in (in_v, in_t, in_q, in_k, load_w):
        load.start()

    barrier = pltpu.get_barrier_semaphore()
    pl.semaphore_signal(barrier, inc=1, device_id=(mate, head), device_id_type=MESH)
    for i in range(heads):
        to = lax.rem(head + i, heads)
        pl.semaphore_signal(barrier, inc=1, device_id=(cross, to), device_id_type=MESH)
        if i:
            pl.semaphore_signal(barrier, inc=1, device_id=(g, to), device_id_type=MESH)
    pl.semaphore_wait(barrier, 2 * heads)

    def remote(src, dst, send_sem, recv_sem, to):
        return pltpu.make_async_remote_copy(
            src_ref=src, dst_ref=dst, send_sem=send_sem, recv_sem=recv_sem, device_id=to, device_id_type=MESH
        )

    def turn_of(i):
        return lax.rem(head + 1 + i, heads)

    def out_q(i):
        chunk = rows(turn_of(i), blocks * BLK)
        return remote(q_h.at[chunk], q_all.at[1, chunk], q_send.at[i], q_recv.at[i], (cross, head))

    out_t = remote(tables.at[1], lists_o, pair_send.at[0], pair_recv.at[0], (cross, head))
    out_v = remote(v_h, v_all.at[mine], pair_send.at[1], pair_recv.at[1], (mate, head))
    out_k = remote(k_h, k_all.at[mine], pair_send.at[2], pair_recv.at[2], (mate, head))
    out_t.start()
    out_v.start()
    out_k.start()
    for i in range(heads):
        out_q(i).start()
    in_v.wait()
    turn_values(v_all, vt, core * per_device, per_device)
    out_t.wait_recv()
    got_t = pltpu.make_async_copy(lists_o, tab.at[1], tab_sem.at[1])
    got_t.start()
    out_v.wait_recv()
    turn_values(v_all, vt, (1 - core) * per_device, per_device)
    in_k.wait()
    in_q.wait()
    in_t.wait()
    got_t.wait()
    out_k.wait_recv()

    def where_is(n):
        i = n // (2 * blocks)
        kind = 1 - n // blocks % 2
        return kind, turn_of(i) * blocks + n % blocks

    def slots_of(kind, b):
        line, at = b // (BLK // ROW), b % (BLK // ROW) * ROW
        ids = [tab[kind, line, at + j] for j in range(SLOTS)]
        bias = [tab[kind, SUBLINES + line, at + j].astype(F32) * -LOW for j in range(SLOTS)]
        return ids, bias

    def score(n, par):
        kind, b = where_is(n)
        ids, bias = slots_of(kind, b)
        return score_slots(q_all[kind, rows(b), :], k_all, s_ref, par, ids, bias)

    def weigh(n, par, top):
        kind, b = where_is(n)
        ids, bias = slots_of(kind, b)
        both = weigh_slots(s_ref, par, vt, ids, bias, top)
        sums = both[BLK : BLK + 8]
        sum0, sum1 = sums[:, :BLK], sums[:, BLK:]
        put_result(done.at[kind], b, both[0:HEAD_DIM, :BLK], both[HEAD_DIM:BLK, BLK:], top, sum0, sum1)

    def out_part(kind, i):
        to = turn_of(i)
        return remote(
            done.at[kind, pl.ds(to * blocks, blocks)], got.at[kind, i],
            part_send.at[kind, i], part_recv.at[kind, i], ((g, cross)[kind], to),
        )

    turns = 2 * heads * blocks // 2
    per_turn = turns // heads

    def pair(j, m0):
        i = j // per_turn
        at = lax.rem(j, per_turn)

        @pl.when(at == per_turn // 2)
        def _():
            out_part(1, i).start()

        @pl.when((at == 0) & (j > 0))
        def _():
            out_part(0, i - 1).start()

        @pl.when((at == per_turn - 1) & (i < heads - 1))
        def _():
            out_q(i + 1).wait_recv()

        n = 2 * j
        m1 = score(n + 1, 1)
        weigh(n, 0, m0)
        m2 = score(jnp.minimum(n + 2, 2 * turns - 1), 0)
        weigh(n + 1, 1, m1)
        return m2

    out_q(0).wait_recv()
    lax.fori_loop(0, turns, pair, score(0, 0))

    def join(i, own):
        out_part(1, i).wait_recv()
        source = lax.rem(head - 1 - i + 2 * heads, heads)
        for b in range(blocks):
            att[pl.ds(b * BLK, BLK), rows(source)] = combine((own(b), got[1, i, b]))

    def join_sent(i, carry):
        out_part(0, i).wait_recv()
        join(i, lambda b: got[0, i, b])
        return carry

    lax.fori_loop(0, heads - 1, join_sent, 0)
    join(heads - 1, lambda b: done[0, head * blocks + b])
    load_w.wait()

    size = blocks * BLK // SUBS

    def back(s, i):
        to = lax.rem(head + i, heads)
        return remote(
            stage.at[to, pl.ds(s * size, size)],
            home.at[pl.ds(pl.multiple_of(head * blocks * BLK, BLK) + s * size, size)],
            back_send.at[s, i], back_recv.at[s, i], (g, to),
        )

    for s in range(SUBS):
        for n in range(0, D, 256):
            out = jnp.dot(att[pl.ds(s * size, size), :], w_ref[:, n : n + 256], preferred_element_type=F32).astype(BF16)
            for c in range(2):
                stage[n // BLK + c, pl.ds(s * size, size), :] = out[:, c * BLK : (c + 1) * BLK]
        for i in range(1, heads):
            back(s, i).start()
        home[pl.ds(pl.multiple_of(head * blocks * BLK, BLK) + s * size, size), :] = stage[head, pl.ds(s * size, size), :]

    out_t.wait_send()
    out_v.wait_send()
    out_k.wait_send()
    for i in range(heads):
        out_q(i).wait_send()
        out_part(1, i).wait_send()
        if i < heads - 1:
            out_part(0, i).wait_send()
    for s in range(SUBS):
        for i in range(1, heads):
            back(s, i).wait()


def mixed_rows(tables, q, k, v, w_out):
    heads = lax.axis_size("head")
    per_device = k.shape[0]
    blocks = q.shape[0] // BLK // heads
    any_ = pl.BlockSpec(memory_space=pl.ANY)
    dma = pltpu.SemaphoreType.DMA
    return pl.pallas_call(
        mixed_kernel,
        out_shape=[jax.ShapeDtypeStruct(q.shape, BF16), jax.ShapeDtypeStruct(tables.shape[1:], I32)],
        in_specs=[any_] * 5,
        out_specs=[pl.BlockSpec(memory_space=pltpu.VMEM), any_],
        scratch_shapes=[
            pltpu.SMEM(tables.shape, I32),
            pltpu.VMEM((2,) + q.shape, BF16),
            pltpu.VMEM((2 * per_device, BLK, BLK), BF16),
            pltpu.VMEM((2 * per_device, BLK, BLK), BF16),
            pltpu.VMEM((2 * per_device, OUT, BLK), BF16),
            pltpu.VMEM((2, SLOTS * BLK, 2 * BLK), F32),
            pltpu.VMEM((2, heads * blocks, OUT, BLK), BF16),
            pltpu.VMEM((2, heads, blocks, OUT, BLK), BF16),
            pltpu.VMEM((blocks * BLK, D), BF16),
            pltpu.VMEM((D, D), BF16),
            pltpu.VMEM((heads, blocks * BLK, BLK), BF16),
            dma((2,)), dma((4,)), dma((3,)), dma((3,)), dma((heads,)), dma((heads,)),
            dma((2, heads)), dma((2, heads)), dma((SUBS, heads)), dma((SUBS, heads)),
        ],
        compiler_params=pltpu.CompilerParams(vmem_limit_bytes=56 << 20, collective_id=0, has_side_effects=True),
        name="mixed_rows",
    )(tables, q, k, v, w_out)[0]


def local(queries, resid, keys, values, w_out, block_lists, block_counts):
    per_device = keys.shape[0] // BLK
    keys, values = keys.reshape(-1, BLK, BLK), values.reshape(-1, BLK, BLK)
    g, core, mate, cross = place()
    used = jnp.arange(SLOTS, dtype=jnp.int32)[None, :] < block_counts[:, None]

    def table(first, count, base):
        here = block_lists - first * per_device
        on = used & (here >= 0) & (here < count * per_device)
        return jnp.stack([jnp.where(on, here + base, 0), 1 - on.astype(jnp.int32)])

    tables = jnp.stack([table(g - core, 2, 0), table(cross, 1, (1 - core) * per_device)])
    tables = jnp.pad(tables, ((0, 0), (0, 0), (0, 0), (0, ROW - SLOTS))).reshape(2, 2 * SUBLINES, BLK)
    home = mixed_rows(tables, queries, keys, values, w_out)
    return (resid.astype(jnp.float32) + home.astype(jnp.float32)).astype(jnp.bfloat16)


def solution(mesh):
    placed = (
        P("grid", "head"),
        P("grid", "head"),
        P("grid", "head"),
        P("grid", "head"),
        P(),
        P("grid", None),
        P("grid"),
    )
    return jax.shard_map(
        local, mesh=mesh, in_specs=placed, out_specs=P("grid", "head"), check_vma=False
    )
```

```python
import functools
import math

import jax
import jax.numpy as jnp
from jax import lax
from jax.experimental import pallas as pl
from jax.experimental.pallas import tpu as pltpu
from jax.sharding import PartitionSpec as P

D = 1024
HEADS = 16
HEAD_DIM = D // HEADS
BLK = 128
SLOTS = 12
ROW = 16
OUT = BLK + 16
LOG2 = math.log2(math.e) / math.sqrt(HEAD_DIM)
LOW = -1e30
SUBLINES = 4
SUBS = 2
PER = 2
UNIT = PER * BLK + 16
CROSS_ORDER = ((0, 1), (1, 3), (0, 2), (1, 1), (0, 3), (1, 0), (1, 2), (0, 0))
OWN_ORDER = ((1, 3), (0, 2), (1, 1), (0, 3), (1, 0), (0, 1), (1, 2), (0, 0))
MIDDLE = 24
BF16, F32, I32 = jnp.bfloat16, jnp.float32, jnp.int32
MESH = pl.DeviceIdType.MESH


def rows(b, size=BLK):
    return pl.ds(pl.multiple_of(b * size, size), size)


def place():
    count = lax.axis_size("grid")
    g = lax.axis_index("grid")
    core = lax.rem(g, 2)
    return g, core, g + 1 - 2 * core, lax.rem(g - 1 + 2 * core + count, count)


def both_heads(q):
    qt = q.T
    row = lax.broadcasted_iota(I32, (BLK, BLK), 0)
    zero = jnp.zeros_like(qt)
    return jnp.concatenate([jnp.where(row < HEAD_DIM, qt, zero), jnp.where(row >= HEAD_DIM, qt, zero)], axis=1)


def score_slots(q, k_ref, s_ref, par, ids, bias):
    q_both = both_heads(q)
    top = None
    for j, (c, less) in enumerate(zip(ids, bias)):
        s = jnp.dot(k_ref[c], q_both, preferred_element_type=F32)
        s_ref[par, pl.ds(j * BLK, BLK), :] = s
        m = jnp.max(s.reshape(BLK // 8, 8, 2 * BLK), axis=0)
        m = m - less
        top = m if top is None else jnp.maximum(top, m)
    top = jnp.max(top, axis=0, keepdims=True) * LOG2
    return top.astype(BF16).astype(F32)


def weigh_slots(s_ref, par, vt, ids, bias, top):
    both = None
    for j in range(0, len(ids), 2):
        w = []
        for i in (j, j + 1):
            shift = top + bias[i]
            w.append(jnp.exp2(s_ref[par, pl.ds(i * BLK, BLK), :] * LOG2 - shift).astype(BF16))
        vals = jnp.concatenate([vt[ids[j]], vt[ids[j + 1]]], axis=1)
        d = jnp.dot(vals, jnp.concatenate(w, axis=0), preferred_element_type=F32)
        both = d if both is None else both + d
    return both


def turn_values(v_ref, vt, first, count):
    def turn(i, carry):
        c = first + i
        vt[c, 0:BLK, :] = v_ref[c].T
        vt[c, BLK:OUT, :] = jnp.ones((OUT - BLK, BLK), BF16)
        return carry

    lax.fori_loop(0, count, turn, 0, unroll=4)


def put_sums(o_ref, at, block, both):
    o_ref[at, block * BLK : block * BLK + HEAD_DIM] = both[0:HEAD_DIM, :BLK].astype(BF16)
    o_ref[at, block * BLK + HEAD_DIM : (block + 1) * BLK] = both[HEAD_DIM:BLK, BLK:].astype(BF16)


def put_stats(o_ref, at, tops, sums):
    row = lax.broadcasted_iota(I32, (16, BLK), 0)
    stats = jnp.zeros((16, BLK), F32)
    for block, (top, total) in enumerate(zip(tops, sums)):
        high = total.astype(BF16).astype(F32)
        for h in range(2):
            part = slice(h * BLK, (h + 1) * BLK)
            for i, line in enumerate((top, high, total - high)):
                stats = jnp.where(row == 6 * block + 3 * h + i, line[0:1, part], stats)
    o_ref[at, PER * BLK : UNIT] = stats.astype(BF16)


def combine(parts, block):
    stats = [p[PER * BLK : UNIT].astype(F32) for p in parts]
    heads = []
    for h in range(2):
        at = 6 * block + 3 * h
        sums = [s[at + 1 : at + 2] + s[at + 2 : at + 3] for s in stats]
        tops = [jnp.where(l > 0, s[at : at + 1], LOW) for s, l in zip(stats, sums)]
        top = functools.reduce(jnp.maximum, tops)
        scale = [jnp.exp2(t - top) for t in tops]
        total = sum(l * c for l, c in zip(sums, scale))
        part = slice(block * BLK + h * HEAD_DIM, block * BLK + (h + 1) * HEAD_DIM)
        heads.append(sum(p[part].astype(F32) * (c / total) for p, c in zip(parts, scale)))
    return jnp.concatenate(heads, axis=0).T.astype(BF16)


def mixed_kernel(
    tables, q_h, k_h, v_h, w_h, resid_h, out, lists_o,
    tab, q_all, k_all, v_all, vt, s_ref, done, got, att, w_ref, stage, home, resid,
    tab_sem, load_sem, out_sem, pair_send, pair_recv, q_send, q_recv, part_send, part_recv, back_send, back_recv,
):
    heads = lax.axis_size("head")
    head = lax.axis_index("head")
    g, core, mate, cross = place()
    per_device = k_h.shape[0]
    blocks = q_h.shape[0] // BLK // heads
    load_w = pltpu.make_async_copy(w_h, w_ref, load_sem.at[0])
    mine = pl.ds(core * per_device, per_device)
    in_v = pltpu.make_async_copy(v_h, v_all.at[mine], load_sem.at[1])
    in_k = pltpu.make_async_copy(k_h, k_all.at[mine], load_sem.at[2])
    in_q = pltpu.make_async_copy(q_h, q_all.at[0], load_sem.at[3])
    in_r = pltpu.make_async_copy(resid_h, resid, load_sem.at[4])
    in_t = pltpu.make_async_copy(tables.at[0], tab.at[0], tab_sem.at[0])
    for load in (in_v, in_t, in_q, in_k, load_w, in_r):
        load.start()

    barrier = pltpu.get_barrier_semaphore()
    pl.semaphore_signal(barrier, inc=1, device_id=(mate, head), device_id_type=MESH)
    for i in range(heads):
        to = lax.rem(head + i, heads)
        pl.semaphore_signal(barrier, inc=1, device_id=(cross, to), device_id_type=MESH)
        if i:
            pl.semaphore_signal(barrier, inc=1, device_id=(g, to), device_id_type=MESH)
    pl.semaphore_wait(barrier, 2 * heads)

    def remote(src, dst, send_sem, recv_sem, to):
        return pltpu.make_async_remote_copy(
            src_ref=src, dst_ref=dst, send_sem=send_sem, recv_sem=recv_sem, device_id=to, device_id_type=MESH
        )

    def turn_of(kind, i):
        x = sum((i == n).astype(I32) * (kind * CROSS_ORDER[n][0] + (1 - kind) * OWN_ORDER[n][0]) for n in range(8))
        z = sum((i == n).astype(I32) * (kind * CROSS_ORDER[n][1] + (1 - kind) * OWN_ORDER[n][1]) for n in range(8))
        return lax.rem(head // 4 + x, 2) * 4 + lax.rem(head % 4 + z, 4)

    def out_q(s, i):
        chunk = rows(turn_of(1, i) * SUBS + s, PER * BLK)
        return remote(q_h.at[chunk], q_all.at[1, chunk], q_send.at[s, i], q_recv.at[s, i], (cross, head))

    out_t = remote(tables.at[1], lists_o, pair_send.at[0], pair_recv.at[0], (cross, head))
    out_v = remote(v_h, v_all.at[mine], pair_send.at[1], pair_recv.at[1], (mate, head))
    out_k = remote(k_h, k_all.at[mine], pair_send.at[2], pair_recv.at[2], (mate, head))
    out_t.start()
    out_v.start()
    out_k.start()
    for s in range(SUBS):
        def send_q(i, carry):
            out_q(s, i).start()
            return carry

        lax.fori_loop(0, heads, send_q, 0)
    in_v.wait()
    turn_values(v_all, vt, core * per_device, per_device)
    out_t.wait_recv()
    got_t = pltpu.make_async_copy(lists_o, tab.at[1], tab_sem.at[1])
    got_t.start()
    out_v.wait_recv()
    turn_values(v_all, vt, (1 - core) * per_device, per_device)
    in_k.wait()
    in_q.wait()
    in_t.wait()
    got_t.wait()
    out_k.wait_recv()

    turns = 2 * heads * SUBS

    def part_of(j):
        i = lax.rem(j // 2, heads)
        kind = 1 - lax.rem(j, 2)
        return kind, j // (2 * heads), i

    def slots_of(kind, b):
        line, at = b // (BLK // ROW), b % (BLK // ROW) * ROW
        ids = [tab[kind, line, at + j] for j in range(SLOTS)]
        bias = [tab[kind, SUBLINES + line, at + j].astype(F32) * -LOW for j in range(SLOTS)]
        return ids, bias

    def score(kind, b, par):
        ids, bias = slots_of(kind, b)
        return score_slots(q_all[kind, rows(b), :], k_all, s_ref, par, ids, bias)

    def weigh(kind, b, par, top, at, block):
        ids, bias = slots_of(kind, b)
        both = weigh_slots(s_ref, par, vt, ids, bias, top)
        put_sums(done.at[kind], at, block, both)
        return both[BLK : BLK + 1]

    def out_part(kind, s, i):
        to = turn_of(kind, i)
        return remote(
            done.at[kind, to * SUBS + s], got.at[kind, s, head],
            part_send.at[kind, s, i], part_recv.at[kind, s, i], ((g, cross)[kind], to),
        )

    size = PER * BLK

    def back(s, i):
        to = lax.rem(head + i, heads)
        return remote(
            stage.at[to, pl.ds(s * size, size)], home.at[head, pl.ds(s * size, size)],
            back_send.at[s, i], back_recv.at[s, i], (g, to),
        )

    def project(s):
        def join(i, carry):
            out_part(1, s, i).wait_recv()
            return carry

        def join_own(i, carry):
            out_part(0, s, i).wait_recv()
            return carry

        lax.fori_loop(0, heads, join, 0)
        lax.fori_loop(0, heads - 1, join_own, 0)

        def mix(source, carry):
            for b in range(PER):
                att[pl.ds(s * size + b * BLK, BLK), rows(source)] = combine(
                    (got.at[0, s, source], got.at[1, s, source]), b
                )
            return carry

        lax.fori_loop(0, heads, mix, 0)
        for n in range(0, D, 256):
            res = jnp.dot(att[pl.ds(s * size, size), :], w_ref[:, n : n + 256], preferred_element_type=F32).astype(BF16)
            for c in range(2):
                stage[n // BLK + c, pl.ds(s * size, size), :] = res[:, c * BLK : (c + 1) * BLK]
        for i in range(1, heads):
            back(s, i).start()

    def pair(j, m0):
        kind, s, i = part_of(j)

        @pl.when(kind == 0)
        def _():
            out_part(1, s, i).start()

        @pl.when((kind == 1) & (i > 0))
        def _():
            out_part(0, s, i - 1).start()

        @pl.when((kind == 1) & (i == 0) & (j > 0))
        def _():
            keep = pltpu.make_async_copy(done.at[0, head * SUBS], got.at[0, 0, head], out_sem.at[0])
            keep.start()
            keep.wait()

        @pl.when(j == MIDDLE)
        def _():
            load_w.wait()
            project(0)

        after = jnp.minimum(j + 1, turns - 1)
        kind2, s2, i2 = part_of(after)

        @pl.when((kind2 == 1) & (j < turns - 1))
        def _():
            out_q(s2, i2).wait_recv()

        to = turn_of(kind, i)
        b = (to * SUBS + s) * PER
        m1 = score(kind, b + 1, 1)
        l0 = weigh(kind, b, 0, m0, to * SUBS + s, 0)
        m2 = score(kind2, (turn_of(kind2, i2) * SUBS + s2) * PER, 0)
        l1 = weigh(kind, b + 1, 1, m1, to * SUBS + s, 1)
        put_stats(done.at[kind], to * SUBS + s, (m0, m1), (l0, l1))
        return m2

    zero = jnp.int32(0)
    out_q(zero, zero).wait_recv()
    lax.fori_loop(0, turns, pair, score(1, turn_of(1, zero) * SUBS * PER, 0))
    keep = pltpu.make_async_copy(done.at[0, head * SUBS + 1], got.at[0, 1, head], out_sem.at[0])
    keep.start()
    keep.wait()
    project(1)

    def finish(s, i):
        source = lax.rem(head - i + heads, heads)
        where = rows(source * SUBS + s, size)
        if i:
            back(s, i).wait_recv()
            come = home[source, pl.ds(s * size, size), :]
        else:
            come = stage[head, pl.ds(s * size, size), :]
        resid[where, :] = (resid[where, :].astype(F32) + come.astype(F32)).astype(BF16)
        return pltpu.make_async_copy(resid.at[where], out.at[where], out_sem.at[s * heads + i])

    in_r.wait()
    for s in range(SUBS):
        for i in range(heads):
            finish_copy = finish(s, i)
            finish_copy.start()

    out_t.wait_send()
    out_v.wait_send()
    out_k.wait_send()

    for s in range(SUBS):
        def sent(i, carry):
            out_q(s, i).wait_send()
            out_part(1, s, i).wait_send()
            return carry

        def sent_own(i, carry):
            out_part(0, s, i).wait_send()
            return carry

        lax.fori_loop(0, heads, sent, 0)
        lax.fori_loop(0, heads - 1, sent_own, 0)
        for i in range(heads):
            if i:
                back(s, i).wait_send()
            source = lax.rem(head - i + heads, heads)
            where = rows(source * SUBS + s, size)
            pltpu.make_async_copy(resid.at[where], out.at[where], out_sem.at[s * heads + i]).wait()


def mixed_rows(tables, q, k, v, w_out, resid):
    heads = lax.axis_size("head")
    per_device = k.shape[0]
    blocks = q.shape[0] // BLK // heads
    any_ = pl.BlockSpec(memory_space=pl.ANY)
    dma = pltpu.SemaphoreType.DMA
    return pl.pallas_call(
        mixed_kernel,
        out_shape=[jax.ShapeDtypeStruct(q.shape, BF16), jax.ShapeDtypeStruct(tables.shape[1:], I32)],
        in_specs=[any_] * 6,
        out_specs=[any_, any_],
        scratch_shapes=[
            pltpu.SMEM(tables.shape, I32),
            pltpu.VMEM((2,) + q.shape, BF16),
            pltpu.VMEM((2 * per_device, BLK, BLK), BF16),
            pltpu.VMEM((2 * per_device, BLK, BLK), BF16),
            pltpu.VMEM((2 * per_device, OUT, BLK), BF16),
            pltpu.VMEM((2, SLOTS * BLK, 2 * BLK), F32),
            pltpu.VMEM((2, heads * SUBS, UNIT, BLK), BF16),
            pltpu.VMEM((2, SUBS, heads, UNIT, BLK), BF16),
            pltpu.VMEM((blocks * BLK, D), BF16),
            pltpu.VMEM((D, D), BF16),
            pltpu.VMEM((heads, blocks * BLK, BLK), BF16),
            pltpu.VMEM((heads, blocks * BLK, BLK), BF16),
            pltpu.VMEM(q.shape, BF16),
            dma((2,)), dma((5,)), dma((SUBS * heads,)), dma((3,)), dma((3,)), dma((SUBS, heads)), dma((SUBS, heads)),
            dma((2, SUBS, heads)), dma((2, SUBS, heads)), dma((SUBS, heads)), dma((SUBS, heads)),
        ],
        compiler_params=pltpu.CompilerParams(vmem_limit_bytes=56 << 20, collective_id=0, has_side_effects=True),
        name="mixed_rows",
    )(tables, q, k, v, w_out, resid)[0]


def local(queries, resid, keys, values, w_out, block_lists, block_counts):
    per_device = keys.shape[0] // BLK
    keys, values = keys.reshape(-1, BLK, BLK), values.reshape(-1, BLK, BLK)
    g, core, mate, cross = place()
    used = jnp.arange(SLOTS, dtype=jnp.int32)[None, :] < block_counts[:, None]

    def table(first, count, base):
        here = block_lists - first * per_device
        on = used & (here >= 0) & (here < count * per_device)
        return jnp.stack([jnp.where(on, here + base, 0), 1 - on.astype(jnp.int32)])

    tables = jnp.stack([table(g - core, 2, 0), table(cross, 1, (1 - core) * per_device)])
    tables = jnp.pad(tables, ((0, 0), (0, 0), (0, 0), (0, ROW - SLOTS))).reshape(2, 2 * SUBLINES, BLK)
    return mixed_rows(tables, queries, keys, values, w_out, resid)


def solution(mesh):
    placed = (
        P("grid", "head"),
        P("grid", "head"),
        P("grid", "head"),
        P("grid", "head"),
        P(),
        P("grid", None),
        P("grid"),
    )
    return jax.shard_map(
        local, mesh=mesh, in_specs=placed, out_specs=P("grid", "head"), check_vma=False
    )
```

```python
import functools
import math

import jax
import jax.numpy as jnp
from jax import lax
from jax.experimental import pallas as pl
from jax.experimental.pallas import tpu as pltpu
from jax.sharding import PartitionSpec as P

D = 1024
HEADS = 16
HEAD_DIM = D // HEADS
BLK = 128
SLOTS = 12
OUT = BLK + 16
LOG2 = math.log2(math.e) / math.sqrt(HEAD_DIM)
LOW = -1e30
SUBS = 2
PER = 2
UNIT = PER * BLK + 16
CROSS_ORDER = ((0, 1), (1, 3), (0, 2), (1, 1), (0, 3), (1, 0), (1, 2), (0, 0))
OWN_ORDER = ((0, 1), (0, 3), (0, 2), (1, 0), (1, 1), (1, 3), (1, 2), (0, 0))
BF16, F32, I32 = jnp.bfloat16, jnp.float32, jnp.int32
MESH = pl.DeviceIdType.MESH


def rows(b, size=BLK):
    return pl.ds(pl.multiple_of(b * size, size), size)


def place():
    count = lax.axis_size("grid")
    g = lax.axis_index("grid")
    core = lax.rem(g, 2)
    return g, core, g + 1 - 2 * core, lax.rem(g - 1 + 2 * core + count, count)


def both_heads(q):
    qt = q.T
    row = lax.broadcasted_iota(I32, (BLK, BLK), 0)
    zero = jnp.zeros_like(qt)
    return jnp.concatenate([jnp.where(row < HEAD_DIM, qt, zero), jnp.where(row >= HEAD_DIM, qt, zero)], axis=1)


def score_slots(q, k_ref, s_ref, par, ids, bias):
    q_both = both_heads(q)
    top = None
    for j, (c, less) in enumerate(zip(ids, bias)):
        s = jnp.dot(k_ref[c], q_both, preferred_element_type=F32)
        s_ref[par, pl.ds(j * BLK, BLK), :] = s
        m = jnp.max(s.reshape(BLK // 8, 8, 2 * BLK), axis=0)
        m = m - less
        top = m if top is None else jnp.maximum(top, m)
    top = jnp.max(top, axis=0, keepdims=True) * LOG2
    return top.astype(BF16).astype(F32)


def weigh_slots(s_ref, par, vt, ids, bias, top):
    both = None
    for j in range(0, len(ids), 2):
        w = []
        for i in (j, j + 1):
            shift = top + bias[i]
            w.append(jnp.exp2(s_ref[par, pl.ds(i * BLK, BLK), :] * LOG2 - shift).astype(BF16))
        vals = jnp.concatenate([vt[ids[j]], vt[ids[j + 1]]], axis=1)
        d = jnp.dot(vals, jnp.concatenate(w, axis=0), preferred_element_type=F32)
        both = d if both is None else both + d
    return both


def turn_values(v_ref, vt, first, count):
    def turn(i, carry):
        c = first + i
        vt[c, 0:BLK, :] = v_ref[c].T
        vt[c, BLK:OUT, :] = jnp.ones((OUT - BLK, BLK), BF16)
        return carry

    lax.fori_loop(0, count, turn, 0, unroll=4)


def put_sums(o_ref, at, block, both):
    o_ref[at, block * BLK : block * BLK + HEAD_DIM] = both[0:HEAD_DIM, :BLK].astype(BF16)
    o_ref[at, block * BLK + HEAD_DIM : (block + 1) * BLK] = both[HEAD_DIM:BLK, BLK:].astype(BF16)


def put_stats(o_ref, at, tops, sums):
    row = lax.broadcasted_iota(I32, (16, BLK), 0)
    stats = jnp.zeros((16, BLK), F32)
    for block, (top, total) in enumerate(zip(tops, sums)):
        high = total.astype(BF16).astype(F32)
        for h in range(2):
            part = slice(h * BLK, (h + 1) * BLK)
            for i, line in enumerate((top, high, total - high)):
                stats = jnp.where(row == 6 * block + 3 * h + i, line[0:1, part], stats)
    o_ref[at, PER * BLK : UNIT] = stats.astype(BF16)


def combine(parts, block):
    stats = [p[PER * BLK : UNIT].astype(F32) for p in parts]
    heads = []
    for h in range(2):
        at = 6 * block + 3 * h
        sums = [s[at + 1 : at + 2] + s[at + 2 : at + 3] for s in stats]
        tops = [jnp.where(l > 0, s[at : at + 1], LOW) for s, l in zip(stats, sums)]
        top = functools.reduce(jnp.maximum, tops)
        scale = [jnp.exp2(t - top) for t in tops]
        total = sum(l * c for l, c in zip(sums, scale))
        part = slice(block * BLK + h * HEAD_DIM, block * BLK + (h + 1) * HEAD_DIM)
        heads.append(sum(p[part].astype(F32) * (c / total) for p, c in zip(parts, scale)))
    return jnp.concatenate(heads, axis=0).T.astype(BF16)


def mixed_kernel(
    lists_h, counts_h, q_h, k_h, v_h, w_h, resid_h, out,
    lists, counts, made, came, tab, q_all, k_all, v_all, vt, s_ref, done, got, att, w_ref, stage, home, resid,
    tab_sem, load_sem, out_sem, pair_send, pair_recv, q_send, q_recv, part_send, part_recv, back_send, back_recv,
):
    heads = lax.axis_size("head")
    head = lax.axis_index("head")
    g, core, mate, cross = place()
    per_device = k_h.shape[0]
    blocks = q_h.shape[0] // BLK // heads
    load_w = pltpu.make_async_copy(w_h, w_ref, load_sem.at[0])
    mine = pl.ds(core * per_device, per_device)
    in_v = pltpu.make_async_copy(v_h, v_all.at[mine], load_sem.at[1])
    in_k = pltpu.make_async_copy(k_h, k_all.at[mine], load_sem.at[2])
    in_q = pltpu.make_async_copy(q_h, q_all.at[0], load_sem.at[3])
    in_r = pltpu.make_async_copy(resid_h, resid, load_sem.at[4])
    in_l = pltpu.make_async_copy(lists_h, lists, tab_sem.at[2])
    in_c = pltpu.make_async_copy(counts_h, counts, tab_sem.at[3])
    for load in (in_l, in_c, in_v, in_q, in_k, load_w, in_r):
        load.start()

    barrier = pltpu.get_barrier_semaphore()
    pl.semaphore_signal(barrier, inc=1, device_id=(mate, head), device_id_type=MESH)
    for i in range(heads):
        to = lax.rem(head + i, heads)
        pl.semaphore_signal(barrier, inc=1, device_id=(cross, to), device_id_type=MESH)
        if i:
            pl.semaphore_signal(barrier, inc=1, device_id=(g, to), device_id_type=MESH)

    made[...] = jnp.zeros_like(made)
    in_l.wait()
    in_c.wait()
    used = lax.broadcasted_iota(I32, lists.shape, 0) < counts[...]
    for n, (first, count, base) in enumerate(((g - core, 2, 0), (cross, 1, (1 - core) * per_device))):
        here = lists[...] - first * per_device
        on = used & (here >= 0) & (here < count * per_device)
        made[n, 0, 0:SLOTS, 0 : lists.shape[1]] = jnp.where(on, here + base, 0)
        made[n, 1, 0:SLOTS, 0 : lists.shape[1]] = jnp.where(on, 0, 1)
    in_t = pltpu.make_async_copy(made.at[0], tab.at[0], tab_sem.at[0])
    in_t.start()
    pl.semaphore_wait(barrier, 2 * heads)

    def remote(src, dst, send_sem, recv_sem, to):
        return pltpu.make_async_remote_copy(
            src_ref=src, dst_ref=dst, send_sem=send_sem, recv_sem=recv_sem, device_id=to, device_id_type=MESH
        )

    def turn_of(kind, i):
        x = sum((i == n).astype(I32) * (kind * CROSS_ORDER[n][0] + (1 - kind) * OWN_ORDER[n][0]) for n in range(8))
        z = sum((i == n).astype(I32) * (kind * CROSS_ORDER[n][1] + (1 - kind) * OWN_ORDER[n][1]) for n in range(8))
        return lax.rem(head // 4 + x, 2) * 4 + lax.rem(head % 4 + z, 4)

    def out_q(s, i):
        chunk = rows(turn_of(1, i) * SUBS + s, PER * BLK)
        return remote(q_h.at[chunk], q_all.at[1, chunk], q_send.at[s, i], q_recv.at[s, i], (cross, head))

    out_t = remote(made.at[1], came, pair_send.at[0], pair_recv.at[0], (cross, head))
    out_v = remote(v_h, v_all.at[mine], pair_send.at[1], pair_recv.at[1], (mate, head))
    out_k = remote(k_h, k_all.at[mine], pair_send.at[2], pair_recv.at[2], (mate, head))
    out_t.start()
    out_v.start()
    out_k.start()
    for s in range(SUBS):
        def send_q(i, carry):
            out_q(s, i).start()
            return carry

        lax.fori_loop(0, heads, send_q, 0)
    in_v.wait()
    turn_values(v_all, vt, core * per_device, per_device)
    out_t.wait_recv()
    got_t = pltpu.make_async_copy(came, tab.at[1], tab_sem.at[1])
    got_t.start()
    out_v.wait_recv()
    turn_values(v_all, vt, (1 - core) * per_device, per_device)
    in_k.wait()
    in_q.wait()
    in_t.wait()
    got_t.wait()
    out_k.wait_recv()

    turns = 2 * heads * SUBS

    def part_of(j):
        s, at = j // (2 * heads), lax.rem(j, 2 * heads)
        third, group = lax.rem(at, 3), at // 3 - 1
        mixed = (at >= 3) & (at < 15)
        kind = (mixed & (third < 2)).astype(I32)
        i = jnp.where(kind == 1, 2 * group + third, jnp.where(mixed, 3 + group, jnp.where(at < 3, at, heads - 1)))
        return kind, s, i

    def slots_of(kind, b):
        ids = [tab[kind, 0, j, b] for j in range(SLOTS)]
        bias = [tab[kind, 1, j, b].astype(F32) * -LOW for j in range(SLOTS)]
        return ids, bias

    def score(kind, b, par):
        ids, bias = slots_of(kind, b)
        return score_slots(q_all[kind, rows(b), :], k_all, s_ref, par, ids, bias)

    def weigh(kind, b, par, top, at, block):
        ids, bias = slots_of(kind, b)
        both = weigh_slots(s_ref, par, vt, ids, bias, top)
        put_sums(done.at[kind], at, block, both)
        return both[BLK : BLK + 1]

    def out_part(kind, s, i):
        to = turn_of(kind, i)
        return remote(
            done.at[kind, to * SUBS + s], got.at[kind, s, head],
            part_send.at[kind, s, i], part_recv.at[kind, s, i], ((g, cross)[kind], to),
        )

    size = PER * BLK

    def back(b, i):
        to = lax.rem(head + i, heads)
        return remote(
            stage.at[to, pl.ds(b * BLK, BLK)], home.at[head, pl.ds(b * BLK, BLK)],
            back_send.at[b, i], back_recv.at[b, i], (g, to),
        )

    def project(s):
        def join(i, carry):
            out_part(1, s, i).wait_recv()
            return carry

        def join_own(i, carry):
            out_part(0, s, i).wait_recv()
            return carry

        lax.fori_loop(0, heads, join, 0)
        lax.fori_loop(0, heads - 1, join_own, 0)

        for n in range(PER):
            b = s * PER + n

            def mix(source, carry):
                att[pl.ds(b * BLK, BLK), rows(source)] = combine((got.at[0, s, source], got.at[1, s, source]), n)
                return carry

            lax.fori_loop(0, heads, mix, 0, unroll=2)
            for c in range(0, heads, 2):
                res = jnp.dot(att[pl.ds(b * BLK, BLK), :], w_ref[:, c * BLK : (c + 2) * BLK], preferred_element_type=F32)
                for d in range(2):
                    stage[c + d, pl.ds(b * BLK, BLK), :] = res[:, d * BLK : (d + 1) * BLK].astype(BF16)
            for i in range(1, heads):
                back(b, i).start()

    def pair(j, m0):
        kind, s, i = part_of(j)

        kind1, s1, i1 = part_of(jnp.maximum(j - 1, 0))

        @pl.when((j > 0) & (kind1 == 1))
        def _():
            out_part(1, s1, i1).start()

        @pl.when((j > 0) & (kind1 == 0) & (i1 < heads - 1))
        def _():
            out_part(0, s1, i1).start()

        @pl.when(j == 2 * heads)
        def _():
            keep = pltpu.make_async_copy(done.at[0, head * SUBS], got.at[0, 0, head], out_sem.at[0])
            keep.start()
            keep.wait()

        after = jnp.minimum(j + 1, turns - 1)
        kind2, s2, i2 = part_of(after)

        @pl.when((kind2 == 1) & (j < turns - 1))
        def _():
            out_q(s2, i2).wait_recv()

        to = turn_of(kind, i)
        b = (to * SUBS + s) * PER
        m1 = score(kind, b + 1, 1)
        l0 = weigh(kind, b, 0, m0, to * SUBS + s, 0)
        m2 = score(kind2, (turn_of(kind2, i2) * SUBS + s2) * PER, 0)
        l1 = weigh(kind, b + 1, 1, m1, to * SUBS + s, 1)
        put_stats(done.at[kind], to * SUBS + s, (m0, m1), (l0, l1))
        return m2

    zero = jnp.int32(0)
    lax.fori_loop(0, turns, pair, score(0, turn_of(0, zero) * SUBS * PER, 0))
    keep = pltpu.make_async_copy(done.at[0, head * SUBS + 1], got.at[0, 1, head], out_sem.at[0])
    keep.start()
    keep.wait()
    load_w.wait()
    project(0)
    project(1)

    def finish(s, i):
        source = lax.rem(head - i + heads, heads)
        where = rows(source * SUBS + s, size)
        if i:
            for n in range(PER):
                back(s * PER + n, i).wait_recv()
            come = home[source, pl.ds(s * size, size), :]
        else:
            come = stage[head, pl.ds(s * size, size), :]
        resid[where, :] = (resid[where, :].astype(F32) + come.astype(F32)).astype(BF16)
        return pltpu.make_async_copy(resid.at[where], out.at[where], out_sem.at[s * heads + i])

    in_r.wait()
    for s in range(SUBS):
        for i in range(heads):
            finish_copy = finish(s, i)
            finish_copy.start()

    out_t.wait_send()
    out_v.wait_send()
    out_k.wait_send()

    for s in range(SUBS):
        def sent(i, carry):
            out_q(s, i).wait_send()
            out_part(1, s, i).wait_send()
            return carry

        def sent_own(i, carry):
            out_part(0, s, i).wait_send()
            return carry

        lax.fori_loop(0, heads, sent, 0)
        lax.fori_loop(0, heads - 1, sent_own, 0)
        for i in range(heads):
            if i:
                for n in range(PER):
                    back(s * PER + n, i).wait_send()
            source = lax.rem(head - i + heads, heads)
            where = rows(source * SUBS + s, size)
            pltpu.make_async_copy(resid.at[where], out.at[where], out_sem.at[s * heads + i]).wait()


def mixed_rows(lists, counts, q, k, v, w_out, resid):
    heads = lax.axis_size("head")
    per_device = k.shape[0]
    blocks = q.shape[0] // BLK // heads
    any_ = pl.BlockSpec(memory_space=pl.ANY)
    dma = pltpu.SemaphoreType.DMA
    return pl.pallas_call(
        mixed_kernel,
        out_shape=jax.ShapeDtypeStruct(q.shape, BF16),
        in_specs=[any_] * 7,
        out_specs=any_,
        scratch_shapes=[
            pltpu.VMEM(lists.shape, I32),
            pltpu.VMEM(counts.shape, I32),
            pltpu.VMEM((2, 2, 16, BLK), I32),
            pltpu.VMEM((2, 16, BLK), I32),
            pltpu.SMEM((2, 2, 16, BLK), I32),
            pltpu.VMEM((2,) + q.shape, BF16),
            pltpu.VMEM((2 * per_device, BLK, BLK), BF16),
            pltpu.VMEM((2 * per_device, BLK, BLK), BF16),
            pltpu.VMEM((2 * per_device, OUT, BLK), BF16),
            pltpu.VMEM((2, SLOTS * BLK, 2 * BLK), F32),
            pltpu.VMEM((2, heads * SUBS, UNIT, BLK), BF16),
            pltpu.VMEM((2, SUBS, heads, UNIT, BLK), BF16),
            pltpu.VMEM((blocks * BLK, D), BF16),
            pltpu.VMEM((D, D), BF16),
            pltpu.VMEM((heads, blocks * BLK, BLK), BF16),
            pltpu.VMEM((heads, blocks * BLK, BLK), BF16),
            pltpu.VMEM(q.shape, BF16),
            dma((4,)), dma((5,)), dma((SUBS * heads,)), dma((3,)), dma((3,)), dma((SUBS, heads)), dma((SUBS, heads)),
            dma((2, SUBS, heads)), dma((2, SUBS, heads)), dma((blocks, heads)), dma((blocks, heads)),
        ],
        compiler_params=pltpu.CompilerParams(vmem_limit_bytes=52 << 20, collective_id=0, has_side_effects=True),
        name="mixed_rows",
    )(lists, counts, q, k, v, w_out, resid)


def local(queries, resid, keys, values, w_out, block_lists, block_counts):
    keys, values = keys.reshape(-1, BLK, BLK), values.reshape(-1, BLK, BLK)
    return mixed_rows(block_lists.T, block_counts[None, :], queries, keys, values, w_out, resid)


def solution(mesh):
    placed = (
        P("grid", "head"),
        P("grid", "head"),
        P("grid", "head"),
        P("grid", "head"),
        P(),
        P("grid", None),
        P("grid"),
    )
    return jax.shard_map(
        local, mesh=mesh, in_specs=placed, out_specs=P("grid", "head"), check_vma=False
    )
```

```python
import functools
import math

import jax
import jax.numpy as jnp
from jax import lax
from jax.experimental import pallas as pl
from jax.experimental.pallas import tpu as pltpu
from jax.sharding import PartitionSpec as P

D = 1024
HEADS = 16
HEAD_DIM = D // HEADS
BLK = 128
SLOTS = 12
OUT = BLK + 16
LOG2 = math.log2(math.e) / math.sqrt(HEAD_DIM)
LOW = -1e30
SUBS = 2
PER = 2
UNIT = PER * BLK + 16
CROSS_ORDER = ((0, 1), (1, 3), (0, 2), (1, 1), (0, 3), (1, 0), (1, 2), (0, 0))
OWN_ORDER = ((0, 1), (0, 3), (0, 2), (1, 0), (1, 1), (1, 3), (1, 2), (0, 0))
BF16, F32, I32 = jnp.bfloat16, jnp.float32, jnp.int32
MESH = pl.DeviceIdType.MESH


def rows(b, size=BLK):
    return pl.ds(pl.multiple_of(b * size, size), size)


def place():
    count = lax.axis_size("grid")
    g = lax.axis_index("grid")
    core = lax.rem(g, 2)
    return g, core, g + 1 - 2 * core, lax.rem(g - 1 + 2 * core + count, count)


def both_heads(q):
    qt = q.T
    row = lax.broadcasted_iota(I32, (BLK, BLK), 0)
    zero = jnp.zeros_like(qt)
    return jnp.concatenate([jnp.where(row < HEAD_DIM, qt, zero), jnp.where(row >= HEAD_DIM, qt, zero)], axis=1)


def score_slots(q, k_ref, s_ref, par, ids, bias):
    q_both = both_heads(q)
    top = None
    for j, (c, less) in enumerate(zip(ids, bias)):
        s = jnp.dot(k_ref[c], q_both, preferred_element_type=F32)
        s_ref[par, pl.ds(j * BLK, BLK), :] = s
        m = jnp.max(s.reshape(BLK // 8, 8, 2 * BLK), axis=0)
        m = m - less
        top = m if top is None else jnp.maximum(top, m)
    top = jnp.max(top, axis=0, keepdims=True) * LOG2
    return top.astype(BF16).astype(F32)


def weigh_slots(s_ref, par, vt, ids, bias, top):
    both = None
    for j in range(0, len(ids), 2):
        w = []
        for i in (j, j + 1):
            shift = top + bias[i]
            w.append(jnp.exp2(s_ref[par, pl.ds(i * BLK, BLK), :] * LOG2 - shift).astype(BF16))
        vals = jnp.concatenate([vt[ids[j]], vt[ids[j + 1]]], axis=1)
        d = jnp.dot(vals, jnp.concatenate(w, axis=0), preferred_element_type=F32)
        both = d if both is None else both + d
    return both


def turn_values(v_ref, vt, first, count):
    def turn(i, carry):
        c = first + i
        vt[c, 0:BLK, :] = v_ref[c].T
        vt[c, BLK:OUT, :] = jnp.ones((OUT - BLK, BLK), BF16)
        return carry

    lax.fori_loop(0, count, turn, 0, unroll=4)


def put_sums(o_ref, at, block, both):
    o_ref[at, block * BLK : block * BLK + HEAD_DIM] = both[0:HEAD_DIM, :BLK].astype(BF16)
    o_ref[at, block * BLK + HEAD_DIM : (block + 1) * BLK] = both[HEAD_DIM:BLK, BLK:].astype(BF16)


def put_stats(o_ref, at, tops, sums):
    row = lax.broadcasted_iota(I32, (16, BLK), 0)
    stats = jnp.zeros((16, BLK), F32)
    for block, (top, total) in enumerate(zip(tops, sums)):
        high = total.astype(BF16).astype(F32)
        for h in range(2):
            part = slice(h * BLK, (h + 1) * BLK)
            for i, line in enumerate((top, high, total - high)):
                stats = jnp.where(row == 6 * block + 3 * h + i, line[0:1, part], stats)
    o_ref[at, PER * BLK : UNIT] = stats.astype(BF16)


def combine(parts, block):
    stats = [p[PER * BLK : UNIT].astype(F32) for p in parts]
    heads = []
    for h in range(2):
        at = 6 * block + 3 * h
        sums = [s[at + 1 : at + 2] + s[at + 2 : at + 3] for s in stats]
        tops = [jnp.where(l > 0, s[at : at + 1], LOW) for s, l in zip(stats, sums)]
        top = functools.reduce(jnp.maximum, tops)
        scale = [jnp.exp2(t - top) for t in tops]
        total = sum(l * c for l, c in zip(sums, scale))
        part = slice(block * BLK + h * HEAD_DIM, block * BLK + (h + 1) * HEAD_DIM)
        heads.append(sum(p[part].astype(F32) * (c / total) for p, c in zip(parts, scale)))
    return jnp.concatenate(heads, axis=0).T.astype(BF16)


def mixed_kernel(
    lists_h, q_h, k_h, v_h, w_h, resid_h, out,
    lists, made, came, tab, q_all, k_all, v_all, vt, s_ref, done, got, att, w_ref, stage, home, resid,
    tab_sem, load_sem, out_sem, pair_send, pair_recv, q_send, q_recv, part_send, part_recv, back_send, back_recv,
):
    heads = lax.axis_size("head")
    head = lax.axis_index("head")
    g, core, mate, cross = place()
    per_device = k_h.shape[0]
    blocks = q_h.shape[0] // BLK // heads
    load_w = pltpu.make_async_copy(w_h, w_ref, load_sem.at[0])
    mine = pl.ds(core * per_device, per_device)
    in_v = pltpu.make_async_copy(v_h, v_all.at[mine], load_sem.at[1])
    in_k = pltpu.make_async_copy(k_h, k_all.at[mine], load_sem.at[2])
    in_q = pltpu.make_async_copy(q_h, q_all.at[0], load_sem.at[3])
    in_r = pltpu.make_async_copy(resid_h, resid, load_sem.at[4])
    in_l = pltpu.make_async_copy(lists_h, lists, tab_sem.at[2])
    barrier = pltpu.get_barrier_semaphore()
    pl.semaphore_signal(barrier, inc=1, device_id=(mate, head), device_id_type=MESH)
    for i in range(heads):
        to = lax.rem(head + i, heads)
        pl.semaphore_signal(barrier, inc=1, device_id=(cross, to), device_id_type=MESH)
        if i:
            pl.semaphore_signal(barrier, inc=1, device_id=(g, to), device_id_type=MESH)

    for load in (in_l, in_v, in_q, in_k, load_w, in_r):
        load.start()

    made[...] = jnp.zeros_like(made)
    in_l.wait()
    listed, counts = lists[0:SLOTS], lists[SLOTS : SLOTS + 1]
    used = lax.broadcasted_iota(I32, listed.shape, 0) < counts
    for n, (first, count, base) in enumerate(((g - core, 2, 0), (cross, 1, (1 - core) * per_device))):
        here = listed - first * per_device
        on = used & (here >= 0) & (here < count * per_device)
        made[n, 0, 0:SLOTS, 0 : lists.shape[1]] = jnp.where(on, here + base, 0)
        made[n, 1, 0:SLOTS, 0 : lists.shape[1]] = jnp.where(on, 0, 1)
    in_t = pltpu.make_async_copy(made.at[0], tab.at[0], tab_sem.at[0])
    in_t.start()
    pl.semaphore_wait(barrier, 2 * heads)

    def remote(src, dst, send_sem, recv_sem, to):
        return pltpu.make_async_remote_copy(
            src_ref=src, dst_ref=dst, send_sem=send_sem, recv_sem=recv_sem, device_id=to, device_id_type=MESH
        )

    def turn_of(kind, i):
        x = sum((i == n).astype(I32) * (kind * CROSS_ORDER[n][0] + (1 - kind) * OWN_ORDER[n][0]) for n in range(8))
        z = sum((i == n).astype(I32) * (kind * CROSS_ORDER[n][1] + (1 - kind) * OWN_ORDER[n][1]) for n in range(8))
        return lax.rem(head // 4 + x, 2) * 4 + lax.rem(head % 4 + z, 4)

    def out_q(s, i):
        chunk = rows(turn_of(1, i) * SUBS + s, PER * BLK)
        return remote(q_h.at[chunk], q_all.at[1, chunk], q_send.at[s, i], q_recv.at[s, i], (cross, head))

    out_t = remote(made.at[1], came, pair_send.at[0], pair_recv.at[0], (cross, head))
    out_v = remote(v_h, v_all.at[mine], pair_send.at[1], pair_recv.at[1], (mate, head))
    out_k = remote(k_h, k_all.at[mine], pair_send.at[2], pair_recv.at[2], (mate, head))
    out_t.start()
    out_v.start()
    out_k.start()
    for s in range(SUBS):
        def send_q(i, carry):
            out_q(s, i).start()
            return carry

        lax.fori_loop(0, heads, send_q, 0)
    in_v.wait()
    turn_values(v_all, vt, core * per_device, per_device)
    out_t.wait_recv()
    got_t = pltpu.make_async_copy(came, tab.at[1], tab_sem.at[1])
    got_t.start()
    out_v.wait_recv()
    turn_values(v_all, vt, (1 - core) * per_device, per_device)
    in_k.wait()
    in_q.wait()
    in_t.wait()
    got_t.wait()
    out_k.wait_recv()

    turns = 2 * heads * SUBS

    def part_of(j):
        s, at = j // (2 * heads), lax.rem(j, 2 * heads)
        third, group = lax.rem(at, 3), at // 3 - 1
        mixed = (at >= 3) & (at < 15)
        kind = (mixed & (third < 2)).astype(I32)
        i = jnp.where(kind == 1, 2 * group + third, jnp.where(mixed, 3 + group, jnp.where(at < 3, at, heads - 1)))
        return kind, s, i

    def slots_of(kind, b):
        ids = [tab[kind, 0, j, b] for j in range(SLOTS)]
        bias = [tab[kind, 1, j, b].astype(F32) * -LOW for j in range(SLOTS)]
        return ids, bias

    def score(kind, b, par):
        ids, bias = slots_of(kind, b)
        return score_slots(q_all[kind, rows(b), :], k_all, s_ref, par, ids, bias)

    def weigh(kind, b, par, top, at, block):
        ids, bias = slots_of(kind, b)
        both = weigh_slots(s_ref, par, vt, ids, bias, top)
        put_sums(done.at[kind], at, block, both)
        return both[BLK : BLK + 1]

    def out_part(kind, s, i):
        to = turn_of(kind, i)
        return remote(
            done.at[kind, to * SUBS + s], got.at[kind, s, head],
            part_send.at[kind, s, i], part_recv.at[kind, s, i], ((g, cross)[kind], to),
        )

    size = PER * BLK

    def back(b, i):
        to = lax.rem(head + i, heads)
        return remote(
            stage.at[to, pl.ds(b * BLK, BLK)], home.at[head, pl.ds(b * BLK, BLK)],
            back_send.at[b, i], back_recv.at[b, i], (g, to),
        )

    def gather(s):
        keep = pltpu.make_async_copy(done.at[0, head * SUBS + s], got.at[0, s, head], out_sem.at[0])
        keep.start()
        keep.wait()
        for i, step in enumerate(CROSS_ORDER):
            own = OWN_ORDER.index(step)
            if own < heads - 1:
                out_part(0, s, jnp.int32(own)).wait_recv()
            out_part(1, s, jnp.int32(i)).wait_recv()
            source = lax.rem(head // 4 + step[0], 2) * 4 + lax.rem(head % 4 - step[1] + 4, 4)
            for n in range(PER):
                att[pl.ds((s * PER + n) * BLK, BLK), rows(source)] = combine(
                    (got.at[0, s, source], got.at[1, s, source]), n
                )

    def project(b):
        for c in range(0, heads, 2):
            res = jnp.dot(att[pl.ds(b * BLK, BLK), :], w_ref[:, c * BLK : (c + 2) * BLK], preferred_element_type=F32)
            for d in range(2):
                stage[c + d, pl.ds(b * BLK, BLK), :] = res[:, d * BLK : (d + 1) * BLK].astype(BF16)

    def send_back(b):
        for i in range(1, heads):
            back(b, i).start()

    def pair(j, m0):
        kind, s, i = part_of(j)

        kind1, s1, i1 = part_of(jnp.maximum(j - 1, 0))

        @pl.when((j > 0) & (kind1 == 1))
        def _():
            out_part(1, s1, i1).start()

        @pl.when((j > 0) & (kind1 == 0) & (i1 < heads - 1))
        def _():
            out_part(0, s1, i1).start()

        after = jnp.minimum(j + 1, turns - 1)
        kind2, s2, i2 = part_of(after)

        @pl.when((kind2 == 1) & (j < turns - 1))
        def _():
            out_q(s2, i2).wait_recv()

        to = turn_of(kind, i)
        b = (to * SUBS + s) * PER
        m1 = score(kind, b + 1, 1)
        l0 = weigh(kind, b, 0, m0, to * SUBS + s, 0)
        m2 = score(kind2, (turn_of(kind2, i2) * SUBS + s2) * PER, 0)
        l1 = weigh(kind, b + 1, 1, m1, to * SUBS + s, 1)
        put_stats(done.at[kind], to * SUBS + s, (m0, m1), (l0, l1))
        return m2

    zero = jnp.int32(0)
    lax.fori_loop(0, turns, pair, score(0, turn_of(0, zero) * SUBS * PER, 0))
    keep = pltpu.make_async_copy(done.at[0, head * SUBS + 1], got.at[0, 1, head], out_sem.at[0])
    keep.start()
    keep.wait()
    load_w.wait()
    for s in range(SUBS):
        gather(s)
        for n in range(PER):
            project(s * PER + n)
            send_back(s * PER + n)

    def finish(s, i):
        source = lax.rem(head - i + heads, heads)
        where = rows(source * SUBS + s, size)
        if i:
            for n in range(PER):
                back(s * PER + n, i).wait_recv()
            come = home[source, pl.ds(s * size, size), :]
        else:
            come = stage[head, pl.ds(s * size, size), :]
        resid[where, :] = (resid[where, :].astype(F32) + come.astype(F32)).astype(BF16)
        return pltpu.make_async_copy(resid.at[where], out.at[where], out_sem.at[s * heads + i])

    in_r.wait()
    for s in range(SUBS):
        for i in range(heads):
            finish_copy = finish(s, i)
            finish_copy.start()

    out_t.wait_send()
    out_v.wait_send()
    out_k.wait_send()

    for s in range(SUBS):
        def sent(i, carry):
            out_q(s, i).wait_send()
            out_part(1, s, i).wait_send()
            return carry

        def sent_own(i, carry):
            out_part(0, s, i).wait_send()
            return carry

        lax.fori_loop(0, heads, sent, 0)
        lax.fori_loop(0, heads - 1, sent_own, 0)
        for i in range(heads):
            if i:
                for n in range(PER):
                    back(s * PER + n, i).wait_send()
            source = lax.rem(head - i + heads, heads)
            where = rows(source * SUBS + s, size)
            pltpu.make_async_copy(resid.at[where], out.at[where], out_sem.at[s * heads + i]).wait()


def mixed_rows(lists, q, k, v, w_out, resid):
    heads = lax.axis_size("head")
    per_device = k.shape[0]
    blocks = q.shape[0] // BLK // heads
    any_ = pl.BlockSpec(memory_space=pl.ANY)
    dma = pltpu.SemaphoreType.DMA
    return pl.pallas_call(
        mixed_kernel,
        out_shape=jax.ShapeDtypeStruct(q.shape, BF16),
        in_specs=[any_] * 6,
        out_specs=any_,
        scratch_shapes=[
            pltpu.VMEM(lists.shape, I32),
            pltpu.VMEM((2, 2, 16, BLK), I32),
            pltpu.VMEM((2, 16, BLK), I32),
            pltpu.SMEM((2, 2, 16, BLK), I32),
            pltpu.VMEM((2,) + q.shape, BF16),
            pltpu.VMEM((2 * per_device, BLK, BLK), BF16),
            pltpu.VMEM((2 * per_device, BLK, BLK), BF16),
            pltpu.VMEM((2 * per_device, OUT, BLK), BF16),
            pltpu.VMEM((2, SLOTS * BLK, 2 * BLK), F32),
            pltpu.VMEM((2, heads * SUBS, UNIT, BLK), BF16),
            pltpu.VMEM((2, SUBS, heads, UNIT, BLK), BF16),
            pltpu.VMEM((blocks * BLK, D), BF16),
            pltpu.VMEM((D, D), BF16),
            pltpu.VMEM((heads, blocks * BLK, BLK), BF16),
            pltpu.VMEM((heads, blocks * BLK, BLK), BF16),
            pltpu.VMEM(q.shape, BF16),
            dma((3,)), dma((5,)), dma((SUBS * heads,)), dma((3,)), dma((3,)), dma((SUBS, heads)), dma((SUBS, heads)),
            dma((2, SUBS, heads)), dma((2, SUBS, heads)), dma((blocks, heads)), dma((blocks, heads)),
        ],
        compiler_params=pltpu.CompilerParams(vmem_limit_bytes=52 << 20, collective_id=0, has_side_effects=True),
        name="mixed_rows",
    )(lists, q, k, v, w_out, resid)


def local(queries, resid, keys, values, w_out, block_lists, block_counts):
    keys, values = keys.reshape(-1, BLK, BLK), values.reshape(-1, BLK, BLK)
    lists = jnp.concatenate([block_lists.T, block_counts[None, :]], axis=0)
    return mixed_rows(lists, queries, keys, values, w_out, resid)


def solution(mesh):
    placed = (
        P("grid", "head"),
        P("grid", "head"),
        P("grid", "head"),
        P("grid", "head"),
        P(),
        P("grid", None),
        P("grid"),
    )
    return jax.shard_map(
        local, mesh=mesh, in_specs=placed, out_specs=P("grid", "head"), check_vma=False
    )
```

```python
import functools
import math

import jax
import jax.numpy as jnp
from jax import lax
from jax.experimental import pallas as pl
from jax.experimental.pallas import tpu as pltpu
from jax.sharding import PartitionSpec as P

D = 1024
HEADS = 16
HEAD_DIM = D // HEADS
BLK = 128
SLOTS = 12
OUT = BLK + 16
LOG2 = math.log2(math.e) / math.sqrt(HEAD_DIM)
LOW = -1e30
SUBS = 2
PER = 2
UNIT = PER * BLK + 16
CROSS_ORDER = ((0, 1), (1, 3), (0, 2), (1, 1), (0, 3), (1, 0), (1, 2), (0, 0))
OWN_ORDER = ((0, 1), (0, 3), (0, 2), (1, 0), (1, 1), (1, 3), (1, 2), (0, 0))
BF16, F32, I32 = jnp.bfloat16, jnp.float32, jnp.int32
MESH = pl.DeviceIdType.MESH


def rows(b, size=BLK):
    return pl.ds(pl.multiple_of(b * size, size), size)


def place():
    count = lax.axis_size("grid")
    g = lax.axis_index("grid")
    core = lax.rem(g, 2)
    return g, core, g + 1 - 2 * core, lax.rem(g - 1 + 2 * core + count, count)


def both_heads(q):
    qt = q.T
    row = lax.broadcasted_iota(I32, (BLK, BLK), 0)
    zero = jnp.zeros_like(qt)
    return jnp.concatenate([jnp.where(row < HEAD_DIM, qt, zero), jnp.where(row >= HEAD_DIM, qt, zero)], axis=1)


def score_slots(q, k_ref, s_ref, par, ids, bias):
    q_both = both_heads(q)
    top = None
    for j, (c, less) in enumerate(zip(ids, bias)):
        s = jnp.dot(k_ref[c], q_both, preferred_element_type=F32)
        s_ref[par, pl.ds(j * BLK, BLK), :] = s
        m = jnp.max(s.reshape(BLK // 8, 8, 2 * BLK), axis=0)
        m = m - less
        top = m if top is None else jnp.maximum(top, m)
    top = jnp.max(top, axis=0, keepdims=True) * LOG2
    return top.astype(BF16).astype(F32)


def weigh_slots(s_ref, par, vt, ids, bias, top):
    both = None
    for j in range(0, len(ids), 2):
        w = []
        for i in (j, j + 1):
            shift = top + bias[i]
            w.append(jnp.exp2(s_ref[par, pl.ds(i * BLK, BLK), :] * LOG2 - shift).astype(BF16))
        vals = jnp.concatenate([vt[ids[j]], vt[ids[j + 1]]], axis=1)
        d = jnp.dot(vals, jnp.concatenate(w, axis=0), preferred_element_type=F32)
        both = d if both is None else both + d
    return both


def turn_values(v_ref, vt, first, count):
    def turn(i, carry):
        c = first + i
        vt[c, 0:BLK, :] = v_ref[c].T
        vt[c, BLK:OUT, :] = jnp.ones((OUT - BLK, BLK), BF16)
        return carry

    lax.fori_loop(0, count, turn, 0, unroll=4)


def put_sums(o_ref, at, block, both):
    o_ref[at, block * BLK : block * BLK + HEAD_DIM] = both[0:HEAD_DIM, :BLK].astype(BF16)
    o_ref[at, block * BLK + HEAD_DIM : (block + 1) * BLK] = both[HEAD_DIM:BLK, BLK:].astype(BF16)


def put_stats(o_ref, at, tops, sums):
    row = lax.broadcasted_iota(I32, (16, BLK), 0)
    stats = jnp.zeros((16, BLK), F32)
    for block, (top, total) in enumerate(zip(tops, sums)):
        high = total.astype(BF16).astype(F32)
        for h in range(2):
            part = slice(h * BLK, (h + 1) * BLK)
            for i, line in enumerate((top, high, total - high)):
                stats = jnp.where(row == 6 * block + 3 * h + i, line[0:1, part], stats)
    o_ref[at, PER * BLK : UNIT] = stats.astype(BF16)


def combine(parts, block):
    stats = [p[PER * BLK : UNIT].astype(F32) for p in parts]
    heads = []
    for h in range(2):
        at = 6 * block + 3 * h
        sums = [s[at + 1 : at + 2] + s[at + 2 : at + 3] for s in stats]
        tops = [jnp.where(l > 0, s[at : at + 1], LOW) for s, l in zip(stats, sums)]
        top = functools.reduce(jnp.maximum, tops)
        scale = [jnp.exp2(t - top) for t in tops]
        total = sum(l * c for l, c in zip(sums, scale))
        part = slice(block * BLK + h * HEAD_DIM, block * BLK + (h + 1) * HEAD_DIM)
        heads.append(sum(p[part].astype(F32) * (c / total) for p, c in zip(parts, scale)))
    return jnp.concatenate(heads, axis=0).T.astype(BF16)


def mixed_kernel(
    lists_h, q_h, k_h, v_h, w_h, resid_h, out,
    lists, made, came, tab, q_all, k_all, v_all, vt, s_ref, done, got, att, w_ref, stage, home, resid,
    tab_sem, load_sem, out_sem, pair_send, pair_recv, q_send, q_recv, part_send, part_recv, back_send, back_recv,
):
    heads = lax.axis_size("head")
    head = lax.axis_index("head")
    g, core, mate, cross = place()
    per_device = k_h.shape[0]
    blocks = q_h.shape[0] // BLK // heads
    load_w = pltpu.make_async_copy(w_h, w_ref, load_sem.at[0])
    mine = pl.ds(core * per_device, per_device)
    in_v = pltpu.make_async_copy(v_h, v_all.at[mine], load_sem.at[1])
    in_k = pltpu.make_async_copy(k_h, k_all.at[mine], load_sem.at[2])
    in_q = pltpu.make_async_copy(q_h, q_all.at[0], load_sem.at[3])
    in_r = pltpu.make_async_copy(resid_h, resid, load_sem.at[4])
    in_l = pltpu.make_async_copy(lists_h, lists, tab_sem.at[2])
    barrier = pltpu.get_barrier_semaphore()
    pl.semaphore_signal(barrier, inc=1, device_id=(mate, head), device_id_type=MESH)
    for i in range(heads):
        to = lax.rem(head + i, heads)
        pl.semaphore_signal(barrier, inc=1, device_id=(cross, to), device_id_type=MESH)
        if i:
            pl.semaphore_signal(barrier, inc=1, device_id=(g, to), device_id_type=MESH)

    for load in (in_l, in_v, in_q, in_k, load_w, in_r):
        load.start()

    made[...] = jnp.zeros_like(made)
    in_l.wait()
    listed, counts = lists[0:SLOTS], lists[SLOTS : SLOTS + 1]
    used = lax.broadcasted_iota(I32, listed.shape, 0) < counts
    for n, (first, count, base) in enumerate(((g - core, 2, 0), (cross, 1, (1 - core) * per_device))):
        here = listed - first * per_device
        on = used & (here >= 0) & (here < count * per_device)
        made[n, 0, 0:SLOTS, 0 : lists.shape[1]] = jnp.where(on, here + base, 0)
        made[n, 1, 0:SLOTS, 0 : lists.shape[1]] = jnp.where(on, 0, 1)
    in_t = pltpu.make_async_copy(made.at[0], tab.at[0], tab_sem.at[0])
    in_t.start()
    pl.semaphore_wait(barrier, 2 * heads)

    def remote(src, dst, send_sem, recv_sem, to):
        return pltpu.make_async_remote_copy(
            src_ref=src, dst_ref=dst, send_sem=send_sem, recv_sem=recv_sem, device_id=to, device_id_type=MESH
        )

    def turn_of(kind, i):
        x = sum((i == n).astype(I32) * (kind * CROSS_ORDER[n][0] + (1 - kind) * OWN_ORDER[n][0]) for n in range(8))
        z = sum((i == n).astype(I32) * (kind * CROSS_ORDER[n][1] + (1 - kind) * OWN_ORDER[n][1]) for n in range(8))
        return lax.rem(head // 4 + x, 2) * 4 + lax.rem(head % 4 + z, 4)

    def out_q(s, i):
        chunk = rows(turn_of(1, i) * SUBS + s, PER * BLK)
        return remote(q_h.at[chunk], q_all.at[1, chunk], q_send.at[s, i], q_recv.at[s, i], (cross, head))

    out_t = remote(made.at[1], came, pair_send.at[0], pair_recv.at[0], (cross, head))
    out_v = remote(v_h, v_all.at[mine], pair_send.at[1], pair_recv.at[1], (mate, head))
    out_k = remote(k_h, k_all.at[mine], pair_send.at[2], pair_recv.at[2], (mate, head))
    out_t.start()

    def send_q(i, s):
        out_q(s, i).start()
        return s

    lax.fori_loop(0, 2, send_q, jnp.int32(0))
    out_v.start()
    out_k.start()
    lax.fori_loop(2, heads, send_q, jnp.int32(0))
    lax.fori_loop(0, heads, send_q, jnp.int32(1))
    in_v.wait()
    turn_values(v_all, vt, core * per_device, per_device)
    out_t.wait_recv()
    got_t = pltpu.make_async_copy(came, tab.at[1], tab_sem.at[1])
    got_t.start()
    out_v.wait_recv()
    turn_values(v_all, vt, (1 - core) * per_device, per_device)
    in_k.wait()
    in_q.wait()
    in_t.wait()
    got_t.wait()
    out_k.wait_recv()

    turns = 2 * heads * SUBS

    def part_of(j):
        s, at = j // (2 * heads), lax.rem(j, 2 * heads)
        third, group = lax.rem(at, 3), at // 3 - 1
        mixed = (at >= 3) & (at < 15)
        kind = (mixed & (third < 2)).astype(I32)
        i = jnp.where(kind == 1, 2 * group + third, jnp.where(mixed, 3 + group, jnp.where(at < 3, at, heads - 1)))
        return kind, s, i

    def slots_of(kind, b):
        ids = [tab[kind, 0, j, b] for j in range(SLOTS)]
        bias = [tab[kind, 1, j, b].astype(F32) * -LOW for j in range(SLOTS)]
        return ids, bias

    def score(kind, b, par):
        ids, bias = slots_of(kind, b)
        return score_slots(q_all[kind, rows(b), :], k_all, s_ref, par, ids, bias)

    def weigh(kind, b, par, top, at, block):
        ids, bias = slots_of(kind, b)
        both = weigh_slots(s_ref, par, vt, ids, bias, top)
        put_sums(done.at[kind], at, block, both)
        return both[BLK : BLK + 1]

    def out_part(kind, s, i):
        to = turn_of(kind, i)
        return remote(
            done.at[kind, to * SUBS + s], got.at[kind, s, head],
            part_send.at[kind, s, i], part_recv.at[kind, s, i], ((g, cross)[kind], to),
        )

    size = PER * BLK

    def back(b, i):
        to = lax.rem(head + i, heads)
        return remote(
            stage.at[to, pl.ds(b * BLK, BLK)], home.at[head, pl.ds(b * BLK, BLK)],
            back_send.at[b, i], back_recv.at[b, i], (g, to),
        )

    def gather(s):
        keep = pltpu.make_async_copy(done.at[0, head * SUBS + s], got.at[0, s, head], out_sem.at[0])
        keep.start()
        keep.wait()
        for i, step in enumerate(CROSS_ORDER):
            own = OWN_ORDER.index(step)
            if own < heads - 1:
                out_part(0, s, jnp.int32(own)).wait_recv()
            out_part(1, s, jnp.int32(i)).wait_recv()
            source = lax.rem(head // 4 + step[0], 2) * 4 + lax.rem(head % 4 - step[1] + 4, 4)
            for n in range(PER):
                att[pl.ds((s * PER + n) * BLK, BLK), rows(source)] = combine(
                    (got.at[0, s, source], got.at[1, s, source]), n
                )

    def project(b):
        for c in range(0, heads, 2):
            res = jnp.dot(att[pl.ds(b * BLK, BLK), :], w_ref[:, c * BLK : (c + 2) * BLK], preferred_element_type=F32)
            for d in range(2):
                stage[c + d, pl.ds(b * BLK, BLK), :] = res[:, d * BLK : (d + 1) * BLK].astype(BF16)

    def send_back(b):
        for i in range(1, heads):
            back(b, i).start()

    def pair(j, m0):
        kind, s, i = part_of(j)

        kind1, s1, i1 = part_of(jnp.maximum(j - 1, 0))

        @pl.when((j > 0) & (kind1 == 1))
        def _():
            out_part(1, s1, i1).start()

        @pl.when((j > 0) & (kind1 == 0) & (i1 < heads - 1))
        def _():
            out_part(0, s1, i1).start()

        after = jnp.minimum(j + 1, turns - 1)
        kind2, s2, i2 = part_of(after)

        @pl.when((kind2 == 1) & (j < turns - 1))
        def _():
            out_q(s2, i2).wait_recv()

        to = turn_of(kind, i)
        b = (to * SUBS + s) * PER
        m1 = score(kind, b + 1, 1)
        l0 = weigh(kind, b, 0, m0, to * SUBS + s, 0)
        m2 = score(kind2, (turn_of(kind2, i2) * SUBS + s2) * PER, 0)
        l1 = weigh(kind, b + 1, 1, m1, to * SUBS + s, 1)
        put_stats(done.at[kind], to * SUBS + s, (m0, m1), (l0, l1))
        return m2

    zero = jnp.int32(0)
    lax.fori_loop(0, turns, pair, score(0, turn_of(0, zero) * SUBS * PER, 0))
    keep = pltpu.make_async_copy(done.at[0, head * SUBS + 1], got.at[0, 1, head], out_sem.at[0])
    keep.start()
    keep.wait()
    load_w.wait()
    for s in range(SUBS):
        gather(s)
        for n in range(PER):
            project(s * PER + n)
            send_back(s * PER + n)

    def keep_rows(b, i):
        source = lax.rem(head - i + heads, heads)
        where = rows(source * blocks + b)
        return source, where, pltpu.make_async_copy(resid.at[where], out.at[where], out_sem.at[b * heads + i])

    in_r.wait()
    for b in range(blocks):
        for i in range(heads):
            source, where, keep = keep_rows(b, i)
            part = pl.ds(b * BLK, BLK)
            if i:
                back(b, i).wait_recv()
            come = home[source, part, :] if i else stage[head, part, :]
            resid[where, :] = (resid[where, :].astype(F32) + come.astype(F32)).astype(BF16)
            keep.start()

    out_t.wait_send()
    out_v.wait_send()
    out_k.wait_send()

    for s in range(SUBS):
        def sent(i, carry):
            out_q(s, i).wait_send()
            out_part(1, s, i).wait_send()
            return carry

        def sent_own(i, carry):
            out_part(0, s, i).wait_send()
            return carry

        lax.fori_loop(0, heads, sent, 0)
        lax.fori_loop(0, heads - 1, sent_own, 0)
    for b in range(blocks):
        for i in range(heads):
            if i:
                back(b, i).wait_send()
            keep_rows(b, i)[2].wait()


def mixed_rows(lists, q, k, v, w_out, resid):
    heads = lax.axis_size("head")
    per_device = k.shape[0]
    blocks = q.shape[0] // BLK // heads
    any_ = pl.BlockSpec(memory_space=pl.ANY)
    dma = pltpu.SemaphoreType.DMA
    return pl.pallas_call(
        mixed_kernel,
        out_shape=jax.ShapeDtypeStruct(q.shape, BF16),
        in_specs=[any_] * 6,
        out_specs=any_,
        scratch_shapes=[
            pltpu.VMEM(lists.shape, I32),
            pltpu.VMEM((2, 2, 16, BLK), I32),
            pltpu.VMEM((2, 16, BLK), I32),
            pltpu.SMEM((2, 2, 16, BLK), I32),
            pltpu.VMEM((2,) + q.shape, BF16),
            pltpu.VMEM((2 * per_device, BLK, BLK), BF16),
            pltpu.VMEM((2 * per_device, BLK, BLK), BF16),
            pltpu.VMEM((2 * per_device, OUT, BLK), BF16),
            pltpu.VMEM((2, SLOTS * BLK, 2 * BLK), F32),
            pltpu.VMEM((2, heads * SUBS, UNIT, BLK), BF16),
            pltpu.VMEM((2, SUBS, heads, UNIT, BLK), BF16),
            pltpu.VMEM((blocks * BLK, D), BF16),
            pltpu.VMEM((D, D), BF16),
            pltpu.VMEM((heads, blocks * BLK, BLK), BF16),
            pltpu.VMEM((heads, blocks * BLK, BLK), BF16),
            pltpu.VMEM(q.shape, BF16),
            dma((3,)), dma((5,)), dma((blocks * heads,)), dma((3,)), dma((3,)), dma((SUBS, heads)), dma((SUBS, heads)),
            dma((2, SUBS, heads)), dma((2, SUBS, heads)), dma((blocks, heads)), dma((blocks, heads)),
        ],
        compiler_params=pltpu.CompilerParams(vmem_limit_bytes=52 << 20, collective_id=0, has_side_effects=True),
        name="mixed_rows",
    )(lists, q, k, v, w_out, resid)


def local(queries, resid, keys, values, w_out, block_lists, block_counts):
    keys, values = keys.reshape(-1, BLK, BLK), values.reshape(-1, BLK, BLK)
    lists = jnp.concatenate([block_lists.T, block_counts[None, :]], axis=0)
    return mixed_rows(lists, queries, keys, values, w_out, resid)


def solution(mesh):
    placed = (
        P("grid", "head"),
        P("grid", "head"),
        P("grid", "head"),
        P("grid", "head"),
        P(),
        P("grid", None),
        P("grid"),
    )
    return jax.shard_map(
        local, mesh=mesh, in_specs=placed, out_specs=P("grid", "head"), check_vma=False
    )
```
